32 devices in a mesh: section: 16 (over z, y, core), tp: 2 (over x).
Axes of the slice: x: 2, y: 2, z: 4, core: 2. Of those that a mesh axis runs over, the one named last changes fastest.
Arguments:
- block_input: bfloat16 [16, 2, 128, 4096], P('section', None, None, 'tp'), may hold values from -6 to 6
- incoming: bfloat16 [16, 2, 128, 4096], P('section', None, None, 'tp'), may hold values from -6 to 6
- in_weight: bfloat16 [16, 4096, 3, 4096], P('section', None, None, 'tp'), may hold values from -0.09375 to 0.09375
- short_taps: float32 [16, 7, 3, 4096], P('section', None, None, 'tp'), may hold values from -2.5 to 2.5
- medium_taps: float32 [16, 128, 256], P('section', None, 'tp'), may hold values from -0.625 to 0.625
- skip_weight: float32 [16, 4096], P('section', 'tp'), may hold values from 0.5 to 1.5
Outputs:
- passed: bfloat16 [16, 2, 128, 4096], P('section', None, None, 'tp')
The draws below stay inside these ranges and needn't reach their ends.
All inputs are finite; a program needn't handle non-finite values.
Results may differ from the reference program's by a relative error of at most 0.0049.
Values may be sent and summed in bfloat16 or wider, within the bound.
No kernel may reach another device: no remote copies, remote signals or barrier semaphores. Data moves between devices by JAX's collectives and lax.ppermute only.
A program may use at most 192 MiB of HBM per device.

```python
import jax
import jax.numpy as jnp
from jax import lax

D = 4096
GROUP = 16
SLEN = 7
MLEN = 128
MB = 2
TOK = 128
SECTIONS = 16


def steps_of(own_key, shape, split, smallest, high):
    def one(dim, shards_of):
        steps = jax.random.uniform(jax.random.fold_in(jax.random.fold_in(own_key, 6), dim), (shards_of,), jnp.float32, smallest / len(split), high / len(split))
        return jnp.repeat(jnp.exp(steps), shape[dim] // shards_of).reshape((-1,) + (1,) * (len(shape) - dim - 1))

    level = one(*split[0])
    for cut in split[1:]:
        level = level * one(*cut)
    return level


def centred(stream_key, extent, deviation, limit, cuts=(), held_as=jnp.bfloat16):
    drawn = deviation * jax.random.normal(stream_key, extent, jnp.float32)
    if cuts:
        drawn = drawn * steps_of(stream_key, extent, cuts, -0.22, 0.18)
    return jnp.clip(drawn, -limit, limit).astype(held_as)


def setup_inputs(seed: int = 0) -> dict:
    splits = jax.random.split(jax.random.key(seed), 7)
    return {
        "block_input": centred(splits[0], (SECTIONS, MB, TOK, D), 1.0, 6.0, ((0, 16), (3, 2))),
        "incoming": centred(splits[1], (SECTIONS, MB, TOK, D), 1.0, 6.0, ((0, 16), (3, 2))),
        "in_weight": centred(splits[2], (SECTIONS, D, 3, D), D ** -0.5, 0.09375, ((0, 16), (3, 2))),
        "short_taps": centred(splits[3], (SECTIONS, SLEN, 3, D), 0.4, 2.5, ((0, 16), (3, 2)), jnp.float32),
        "medium_taps": centred(splits[4], (SECTIONS, MLEN, D // GROUP), 0.1, 0.625, ((0, 16), (2, 2)), jnp.float32),
        "skip_weight": jnp.clip(0.5 + 1.0 * jax.random.uniform(splits[5], (SECTIONS, D), jnp.float32) ** steps_of(splits[5], (SECTIONS, D), ((0, 16), (1, 2)), -0.2, 0.2), 0.5, 1.5),
    }


def causal_taps(series, taps):
    length = series.shape[1]
    reach = taps.shape[0]
    padded = jnp.pad(series, ((0, 0), (reach - 1, 0), (0, 0), (0, 0)))
    result = jnp.zeros(series.shape, jnp.float32)
    for offset in range(reach):
        first = reach - 1 - offset
        result = result + taps[offset] * padded[:, first:first + length]
    return result

def anti_taps(series, taps):
    length = series.shape[1]
    reach = taps.shape[0]
    padded = jnp.pad(series, ((0, 0), (0, reach - 1), (0, 0), (0, 0)))
    result = jnp.zeros(series.shape, jnp.float32)
    for offset in range(reach):
        result = result + taps[offset] * padded[:, offset:offset + length]
    return result

def toeplitz_of(medium, length):
    places = jnp.arange(length, dtype=jnp.int32)
    lag_table = places[:, None] - places[None, :]
    lag_values = jnp.arange(medium.shape[0], dtype=jnp.int32)
    lag_match = (lag_table[:, :, None] == lag_values[None, None, :]).astype(jnp.float32)
    return jnp.einsum('tsj,jg->tsg', lag_match, medium, precision=lax.Precision.HIGHEST)

def section_grad(block_input, incoming, in_weight, short_taps, medium_taps, skip_weight):
    micro_count, length, model_width = block_input.shape
    groups = medium_taps.shape[1]
    weights = in_weight.reshape(model_width, 3 * model_width)
    flattened = block_input.reshape(micro_count * length, model_width)
    projected = jnp.dot(flattened, weights, preferred_element_type=jnp.float32)
    projected = projected.reshape(micro_count, length, 3, model_width)
    featured = causal_taps(projected, short_taps)
    query = featured[:, :, 0]
    key_part = featured[:, :, 1]
    value_part = featured[:, :, 2]
    product = key_part * value_part
    toeplitz_mat = toeplitz_of(medium_taps, length)
    grouped = product.reshape(micro_count, length, groups, -1)
    mixed = jnp.einsum('tsg,bsgc->btgc', toeplitz_mat, grouped, precision=lax.Precision.HIGHEST)
    mixed = mixed.reshape(micro_count, length, model_width) + skip_weight * product
    upstream = incoming.astype(jnp.float32)
    query_grad = upstream * mixed
    mixed_grad = upstream * query
    grouped_grad = mixed_grad.reshape(micro_count, length, groups, -1)
    product_grad = jnp.einsum('tsg,btgc->bsgc', toeplitz_mat, grouped_grad, precision=lax.Precision.HIGHEST)
    product_grad = product_grad.reshape(micro_count, length, model_width) + skip_weight * mixed_grad
    stream_grad = jnp.stack([query_grad, product_grad * value_part, product_grad * key_part], axis=2)
    conv_grad = anti_taps(stream_grad, short_taps).astype(jnp.bfloat16)
    conv_flat = conv_grad.reshape(micro_count * length, 3 * model_width)
    input_grad = lax.dot_general(conv_flat, weights, (((1,), (1,)), ((), ())), preferred_element_type=jnp.float32)
    input_grad = input_grad.reshape(micro_count, length, model_width)
    return (upstream + input_grad).astype(jnp.bfloat16)

def reference(block_input, incoming, in_weight, short_taps, medium_taps, skip_weight):

    def one_section(bundle):
        return section_grad(*bundle)
    results = lax.map(one_section, (block_input, incoming, in_weight, short_taps, medium_taps, skip_weight))
    return jnp.roll(results, -1, axis=0)
```

```python
import functools

import jax
import jax.numpy as jnp
from jax import lax
from jax.experimental import pallas as pl
from jax.experimental.pallas import tpu as pltpu
from jax.sharding import PartitionSpec as P

F32 = jnp.float32
BF16 = jnp.bfloat16
LANES = 128
VMEM_LIMIT = 56 * 1024 * 1024


def params(semantics):
    return pltpu.CompilerParams(
        dimension_semantics=semantics, vmem_limit_bytes=VMEM_LIMIT
    )


def cost(flops, moved):
    return pl.CostEstimate(flops=flops, bytes_accessed=moved, transcendentals=0)


def project_kernel(owner_ref, x_ref, w_ref, *rest):
    out_ref = rest[-1]
    total = jnp.dot(x_ref[...], w_ref[0], preferred_element_type=F32)
    if len(rest) > 1:
        total = total + rest[0][0]
    out_ref[0] = total


def project(x, weights, owner, so_far=None):
    rows, depth = x.shape
    channels = weights.shape[2]
    width = min(512, channels)
    block = pl.BlockSpec((1, rows, width), lambda i, j, o: (i, 0, j))
    in_specs = [
        pl.BlockSpec((rows, depth), lambda i, j, o: (0, 0)),
        pl.BlockSpec((1, depth, width), lambda i, j, o: (i, o[0], j)),
    ]
    operands = [x, weights]
    if so_far is not None:
        in_specs.append(block)
        operands.append(so_far)
    return pl.pallas_call(
        project_kernel,
        grid_spec=pltpu.PrefetchScalarGridSpec(
            num_scalar_prefetch=1,
            grid=(3, channels // width),
            in_specs=in_specs,
            out_specs=block,
        ),
        out_shape=jax.ShapeDtypeStruct((3, rows, channels), F32),
        compiler_params=params(("arbitrary", "arbitrary")),
        cost_estimate=cost(6 * rows * depth * channels, 6 * depth * channels + 12 * rows * channels),
        name="project",
    )(owner, *operands)


def toeplitz_kernel(taps_ref, turned_ref, first_ref, second_ref):
    length = first_ref.shape[0]
    count = taps_ref.shape[0]
    rows = lax.broadcasted_iota(jnp.int32, (length, length), 0)
    columns = lax.broadcasted_iota(jnp.int32, (length, length), 1)
    for g in range(count):
        place = slice(g * length, (g + 1) * length)
        base = jnp.broadcast_to(turned_ref[g : g + 1, :], (length, length))
        rolled = pltpu.roll(base, 0, 1, stride=1, stride_axis=0)
        first_ref[:, place] = jnp.where(columns <= rows, rolled, 0.0).astype(BF16)
        base = jnp.broadcast_to(taps_ref[g : g + 1, :], (length, length))
        rolled = pltpu.roll(base, 0, 1, stride=1, stride_axis=0)
        second_ref[:, place] = jnp.where(columns >= rows, rolled, 0.0).astype(BF16)


def toeplitz_pair(medium):
    reach, groups = medium.shape
    taps = medium.T
    turned = jnp.concatenate([taps[:, :1], taps[:, :0:-1]], axis=1)
    step = 8
    shape = jax.ShapeDtypeStruct((reach, groups * reach), BF16)
    row = pl.BlockSpec((step, reach), lambda g: (g, 0))
    block = pl.BlockSpec((reach, step * reach), lambda g: (0, g))
    return pl.pallas_call(
        toeplitz_kernel,
        grid=(groups // step,),
        in_specs=[row, row],
        out_specs=[block, block],
        out_shape=[shape, shape],
        compiler_params=params(("arbitrary",)),
        cost_estimate=cost(0, 4 * groups * reach * reach),
        name="toeplitz",
    )(taps, turned)


def down(series, steps):
    moved = pltpu.roll(series, steps, 0)
    row = lax.broadcasted_iota(jnp.int32, (8, series.shape[1]), 0)
    return jnp.concatenate([jnp.where(row >= steps, moved[:8], 0.0), moved[8:]], axis=0)


def up(series, steps):
    length = series.shape[0]
    moved = pltpu.roll(series, length - steps, 0)
    row = lax.broadcasted_iota(jnp.int32, (8, series.shape[1]), 0)
    last = jnp.where(row < 8 - steps, moved[length - 8 :], 0.0)
    return jnp.concatenate([moved[: length - 8], last], axis=0)


def short_filter(series, taps, move):
    shifted = [series] + [move(series, steps) for steps in range(1, 4)]
    near = taps[0] * series
    far = None
    for lag in range(1, len(taps)):
        term = taps[lag] * shifted[lag % 4]
        if lag < 4:
            near = near + term
        else:
            far = term if far is None else far + term
    if far is None:
        return near
    return near + move(far, 4)


def group_masks(members, width):
    group = lax.broadcasted_iota(jnp.int32, (1, width), 1) % LANES // members
    return [jnp.where(group == g, 1.0, 0.0).astype(BF16) for g in range(LANES // members)]


def medium_filter(toeplitz, series, masks):
    rounded = series.astype(BF16)
    stacked = jnp.concatenate([rounded * mask for mask in masks], axis=0)
    return jnp.dot(toeplitz, stacked, preferred_element_type=F32)


def mixer_kernel(
    owner_ref, x_ref, w_ref, so_far_ref, first_ref, second_ref, taps_ref, skip_ref, grad_ref,
    out_ref, *, micro, members
):
    rows, width = out_ref.shape[1:]
    length = rows // micro
    spread = LANES // members * length
    masks = group_masks(members, micro * LANES)
    x = x_ref[...]
    projected = [
        jnp.dot(x, w_ref[i], preferred_element_type=F32) + so_far_ref[i] for i in range(3)
    ]
    for tile in range(width // LANES):
        lanes = slice(tile * LANES, (tile + 1) * LANES)
        taps = [[taps_ref[j, i : i + 1, lanes] for j in range(taps_ref.shape[0])] for i in range(3)]
        skip = skip_ref[0:1, lanes]
        window = slice(tile * spread, (tile + 1) * spread)
        query, key, value, upstream = [], [], [], []
        for b in range(micro):
            span = slice(b * length, (b + 1) * length)
            series = [short_filter(projected[i][span, lanes], taps[i], down) for i in range(3)]
            query.append(series[0])
            key.append(series[1])
            value.append(series[2])
            upstream.append(grad_ref[span, lanes].astype(F32))
        product = [k * v for k, v in zip(key, value)]
        mixed = medium_filter(first_ref[:, window], jnp.concatenate(product, axis=1), masks)
        mixed_grad = [u * q for u, q in zip(upstream, query)]
        product_grad = medium_filter(
            second_ref[:, window], jnp.concatenate(mixed_grad, axis=1), masks
        )
        for b in range(micro):
            span = slice(b * length, (b + 1) * length)
            part = slice(b * LANES, (b + 1) * LANES)
            back = product_grad[:, part] + skip * mixed_grad[b]
            grads = [
                upstream[b] * (mixed[:, part] + skip * product[b]),
                back * value[b],
                back * key[b],
            ]
            for i in range(3):
                out_ref[i, span, lanes] = short_filter(grads[i], taps[i], up).astype(BF16)


def mixer(x, weights, owner, so_far, first, second, taps, skip, grad, micro):
    rows, depth = x.shape
    channels = weights.shape[2]
    length = rows // micro
    groups = first.shape[1] // length
    members = channels // groups
    width = min(256, channels)
    spread = width // members * length
    block = pl.BlockSpec((3, rows, width), lambda j, o: (0, 0, j))
    matrix = pl.BlockSpec((length, spread), lambda j, o: (0, j))
    return pl.pallas_call(
        functools.partial(mixer_kernel, micro=micro, members=members),
        grid_spec=pltpu.PrefetchScalarGridSpec(
            num_scalar_prefetch=1,
            grid=(channels // width,),
            in_specs=[
                pl.BlockSpec((rows, depth), lambda j, o: (0, 0)),
                pl.BlockSpec((3, depth, width), lambda j, o: (0, o[0], j)),
                block,
                matrix,
                matrix,
                pl.BlockSpec((taps.shape[0], 3, width), lambda j, o: (0, 0, j)),
                pl.BlockSpec((1, width), lambda j, o: (0, j)),
                pl.BlockSpec((rows, width), lambda j, o: (0, j)),
            ],
            out_specs=block,
        ),
        out_shape=jax.ShapeDtypeStruct((3, rows, channels), BF16),
        compiler_params=params(("arbitrary",)),
        cost_estimate=cost(6 * rows * depth * channels, 6 * depth * channels + 18 * rows * channels),
        name="mixer",
    )(owner, x, weights, so_far, first, second, taps, skip, grad)


def input_grad_kernel(member_ref, conv_ref, w_ref, *rest):
    out_ref = rest[-1]
    total = rest[0][...].astype(F32) if len(rest) > 1 else None
    for i in range(3):
        term = lax.dot_general(
            conv_ref[i], w_ref[i], (((1,), (1,)), ((), ())), preferred_element_type=F32
        )
        total = term if total is None else total + term
    out_ref[...] = total.astype(BF16)


def input_grad(conv, weights, member, part, parts, depth, grad=None):
    rows, channels = conv.shape[1:]
    extent = depth // parts
    width = min(256, extent)
    steps = extent // width
    in_specs = [
        pl.BlockSpec((3, rows, channels), lambda j, m: (0, 0, 0)),
        pl.BlockSpec((3, width, channels), lambda j, m: (0, (m[0] * parts + part) * steps + j, 0)),
    ]
    operands = [conv, weights]
    if grad is not None:
        in_specs.append(pl.BlockSpec((rows, width), lambda j, m: (0, part * steps + j)))
        operands.append(grad)
    return pl.pallas_call(
        input_grad_kernel,
        grid_spec=pltpu.PrefetchScalarGridSpec(
            num_scalar_prefetch=1,
            grid=(steps,),
            in_specs=in_specs,
            out_specs=pl.BlockSpec((rows, width), lambda j, m: (0, j)),
        ),
        out_shape=jax.ShapeDtypeStruct((rows, extent), BF16),
        compiler_params=params(("arbitrary",)),
        cost_estimate=cost(6 * rows * extent * channels, 6 * extent * channels + 8 * rows * channels),
        name="input_grad",
    )(member, *operands)


def join(pieces):
    rows, extent = pieces[0][0].shape
    flat = [piece for part in pieces for piece in part]
    sources = len(pieces[0])

    def kernel(*refs):
        out_ref = refs[-1]
        for p in range(len(pieces)):
            total = refs[p * sources][...].astype(F32)
            for s in range(1, sources):
                total = total + refs[p * sources + s][...].astype(F32)
            out_ref[:, p * extent : (p + 1) * extent] = total.astype(BF16)

    return pl.pallas_call(
        kernel,
        out_shape=jax.ShapeDtypeStruct((rows, extent * len(pieces)), BF16),
        compiler_params=pltpu.CompilerParams(vmem_limit_bytes=VMEM_LIMIT),
        cost_estimate=cost(0, 2 * rows * extent * (len(flat) + len(pieces))),
        name="join",
    )(*flat)


PARTS = 2


def local(block_input, incoming, in_weight, short_taps, medium_taps, skip_weight):
    micro, length, depth = block_input.shape[1:]
    rows = micro * length
    members = lax.axis_size("tp")
    sections = lax.axis_size("section")
    me = lax.axis_index("tp")
    weights = jnp.transpose(in_weight[0], (1, 0, 2))
    x = block_input.reshape(rows, depth)
    grad = incoming.reshape(rows, depth)

    def owner(step):
        return jnp.full((1,), lax.rem(me + step, members), jnp.int32)

    from_member = [x]
    for k in range(1, members):
        pairs = [((m + k) % members, m) for m in range(members)]
        from_member.append(lax.ppermute(x, "tp", pairs))
    so_far = None
    for k in range(members - 1):
        so_far = project(from_member[k], weights, owner(k), so_far)
    first, second = toeplitz_pair(medium_taps[0])
    conv = mixer(
        from_member[-1], weights, owner(members - 1), so_far, first, second,
        short_taps[0], skip_weight, grad, micro,
    )
    pieces = [[None] * members for _ in range(PARTS)]
    for k in list(range(1, members)) + [0]:
        pairs = [
            (s * members + m, (s - 1) % sections * members + (m + k) % members)
            for s in range(sections)
            for m in range(members)
        ]
        for part in range(PARTS):
            share = input_grad(
                conv, weights, owner(k), part, PARTS, depth, grad if k == 0 else None
            )
            pieces[part][k] = lax.ppermute(share, ("section", "tp"), pairs)
    return join(pieces).reshape(block_input.shape)


def solution(mesh):
    in_specs = (
        P("section", None, None, "tp"),
        P("section", None, None, "tp"),
        P("section", None, None, "tp"),
        P("section", None, None, "tp"),
        P("section", None, "tp"),
        P("section", "tp"),
    )
    out_specs = P("section", None, None, "tp")
    return jax.shard_map(local, mesh=mesh, in_specs=in_specs, out_specs=out_specs, check_vma=False)
```

```python
import functools

import jax
import jax.numpy as jnp
from jax import lax
from jax.experimental import pallas as pl
from jax.experimental.pallas import tpu as pltpu
from jax.sharding import PartitionSpec as P

F32 = jnp.float32
BF16 = jnp.bfloat16
LANES = 128
VMEM_LIMIT = 56 * 1024 * 1024


def params(semantics):
    return pltpu.CompilerParams(
        dimension_semantics=semantics, vmem_limit_bytes=VMEM_LIMIT
    )


def cost(flops, moved):
    return pl.CostEstimate(flops=flops, bytes_accessed=moved, transcendentals=0)


def project_kernel(owner_ref, x_ref, *rest, spans):
    out_ref = rest[-1]
    depth = x_ref.shape[1] // spans
    total = rest[spans][0] if len(rest) > spans + 1 else None
    for k in range(spans):
        term = jnp.dot(
            x_ref[:, k * depth : (k + 1) * depth], rest[k][0], preferred_element_type=F32
        )
        total = term if total is None else total + term
    out_ref[0] = total


def project(x, weights, owner, so_far=None):
    rows, depth = x.shape
    channels = weights.shape[2]
    width = min(512, channels)
    spans = 4 if depth >= 1024 else 1
    block = pl.BlockSpec((1, rows, width), lambda i, j, o: (i, 0, j))
    in_specs = [pl.BlockSpec((rows, depth), lambda i, j, o: (0, 0))]
    for k in range(spans):
        in_specs.append(
            pl.BlockSpec(
                (1, depth // spans, width),
                lambda i, j, o, k=k: (i, o[0] * spans + k, j),
            )
        )
    operands = [x] + [weights] * spans
    if so_far is not None:
        in_specs.append(block)
        operands.append(so_far)
    return pl.pallas_call(
        functools.partial(project_kernel, spans=spans),
        grid_spec=pltpu.PrefetchScalarGridSpec(
            num_scalar_prefetch=1,
            grid=(3, channels // width),
            in_specs=in_specs,
            out_specs=block,
        ),
        out_shape=jax.ShapeDtypeStruct((3, rows, channels), F32),
        compiler_params=params(("arbitrary", "arbitrary")),
        cost_estimate=cost(6 * rows * depth * channels, 6 * depth * channels + 12 * rows * channels),
        name="project",
    )(owner, *operands)


def toeplitz_kernel(taps_ref, turned_ref, first_ref, second_ref):
    length = first_ref.shape[0]
    count = taps_ref.shape[0]
    rows = lax.broadcasted_iota(jnp.int32, (length, length), 0)
    columns = lax.broadcasted_iota(jnp.int32, (length, length), 1)
    for g in range(count):
        place = slice(g * length, (g + 1) * length)
        base = jnp.broadcast_to(turned_ref[g : g + 1, :], (length, length))
        rolled = pltpu.roll(base, 0, 1, stride=1, stride_axis=0)
        first_ref[:, place] = jnp.where(columns <= rows, rolled, 0.0).astype(BF16)
        base = jnp.broadcast_to(taps_ref[g : g + 1, :], (length, length))
        rolled = pltpu.roll(base, 0, 1, stride=1, stride_axis=0)
        second_ref[:, place] = jnp.where(columns >= rows, rolled, 0.0).astype(BF16)


def toeplitz_pair(medium):
    reach, groups = medium.shape
    taps = medium.T
    turned = jnp.concatenate([taps[:, :1], taps[:, :0:-1]], axis=1)
    step = 8
    shape = jax.ShapeDtypeStruct((reach, groups * reach), BF16)
    row = pl.BlockSpec((step, reach), lambda g: (g, 0))
    block = pl.BlockSpec((reach, step * reach), lambda g: (0, g))
    return pl.pallas_call(
        toeplitz_kernel,
        grid=(groups // step,),
        in_specs=[row, row],
        out_specs=[block, block],
        out_shape=[shape, shape],
        compiler_params=params(("arbitrary",)),
        cost_estimate=cost(0, 4 * groups * reach * reach),
        name="toeplitz",
    )(taps, turned)


def down(series, steps):
    moved = pltpu.roll(series, steps, 0)
    row = lax.broadcasted_iota(jnp.int32, (8, series.shape[1]), 0)
    return jnp.concatenate([jnp.where(row >= steps, moved[:8], 0.0), moved[8:]], axis=0)


def up(series, steps):
    length = series.shape[0]
    moved = pltpu.roll(series, length - steps, 0)
    row = lax.broadcasted_iota(jnp.int32, (8, series.shape[1]), 0)
    last = jnp.where(row < 8 - steps, moved[length - 8 :], 0.0)
    return jnp.concatenate([moved[: length - 8], last], axis=0)


def short_filter(series, taps, move):
    shifted = [series] + [move(series, steps) for steps in range(1, 4)]
    near = taps[0] * series
    far = None
    for lag in range(1, len(taps)):
        term = taps[lag] * shifted[lag % 4]
        if lag < 4:
            near = near + term
        else:
            far = term if far is None else far + term
    if far is None:
        return near
    return near + move(far, 4)


def group_masks(members, width):
    group = lax.broadcasted_iota(jnp.int32, (1, width), 1) % LANES // members
    return [jnp.where(group == g, 1.0, 0.0).astype(BF16) for g in range(LANES // members)]


def medium_filter(toeplitz, series, masks):
    rounded = series.astype(BF16)
    stacked = jnp.concatenate([rounded * mask for mask in masks], axis=0)
    return jnp.dot(toeplitz, stacked, preferred_element_type=F32)


def mixer_kernel(
    owner_ref, x_ref, w0_ref, w1_ref, w2_ref, so_far_ref, first_ref, second_ref, taps_ref,
    skip_ref, grad_ref, out_ref, *, micro, members
):
    rows, width = out_ref.shape[1:]
    length = rows // micro
    spread = LANES // members * length
    masks = group_masks(members, micro * LANES)
    x = x_ref[...]
    projected = [
        jnp.dot(x, w_ref[0], preferred_element_type=F32) + so_far_ref[i]
        for i, w_ref in enumerate((w0_ref, w1_ref, w2_ref))
    ]
    for tile in range(width // LANES):
        lanes = slice(tile * LANES, (tile + 1) * LANES)
        taps = [[taps_ref[j, i : i + 1, lanes] for j in range(taps_ref.shape[0])] for i in range(3)]
        skip = skip_ref[0:1, lanes]
        window = slice(tile * spread, (tile + 1) * spread)
        query, key, value, upstream = [], [], [], []
        for b in range(micro):
            span = slice(b * length, (b + 1) * length)
            series = [short_filter(projected[i][span, lanes], taps[i], down) for i in range(3)]
            query.append(series[0])
            key.append(series[1])
            value.append(series[2])
            upstream.append(grad_ref[span, lanes].astype(F32))
        product = [k * v for k, v in zip(key, value)]
        mixed = medium_filter(first_ref[:, window], jnp.concatenate(product, axis=1), masks)
        mixed_grad = [u * q for u, q in zip(upstream, query)]
        product_grad = medium_filter(
            second_ref[:, window], jnp.concatenate(mixed_grad, axis=1), masks
        )
        for b in range(micro):
            span = slice(b * length, (b + 1) * length)
            part = slice(b * LANES, (b + 1) * LANES)
            back = product_grad[:, part] + skip * mixed_grad[b]
            grads = [
                upstream[b] * (mixed[:, part] + skip * product[b]),
                back * value[b],
                back * key[b],
            ]
            for i in range(3):
                out_ref[i, span, lanes] = short_filter(grads[i], taps[i], up).astype(BF16)


def mixer(x, weights, owner, so_far, first, second, taps, skip, grad, micro):
    rows, depth = x.shape
    channels = weights.shape[2]
    length = rows // micro
    groups = first.shape[1] // length
    members = channels // groups
    width = min(256, channels)
    spread = width // members * length
    block = pl.BlockSpec((3, rows, width), lambda j, o: (0, 0, j))
    matrix = pl.BlockSpec((length, spread), lambda j, o: (0, j))
    return pl.pallas_call(
        functools.partial(mixer_kernel, micro=micro, members=members),
        grid_spec=pltpu.PrefetchScalarGridSpec(
            num_scalar_prefetch=1,
            grid=(channels // width,),
            in_specs=[
                pl.BlockSpec((rows, depth), lambda j, o: (0, 0)),
                *[
                    pl.BlockSpec((1, depth, width), lambda j, o, i=i: (i, o[0], j))
                    for i in range(3)
                ],
                block,
                matrix,
                matrix,
                pl.BlockSpec((taps.shape[0], 3, width), lambda j, o: (0, 0, j)),
                pl.BlockSpec((1, width), lambda j, o: (0, j)),
                pl.BlockSpec((rows, width), lambda j, o: (0, j)),
            ],
            out_specs=block,
        ),
        out_shape=jax.ShapeDtypeStruct((3, rows, channels), BF16),
        compiler_params=params(("arbitrary",)),
        cost_estimate=cost(6 * rows * depth * channels, 6 * depth * channels + 18 * rows * channels),
        name="mixer",
    )(owner, x, weights, weights, weights, so_far, first, second, taps, skip, grad)


def input_grad_kernel(member_ref, conv_ref, w0_ref, w1_ref, w2_ref, *rest):
    out_ref = rest[-1]
    total = None
    for i, w_ref in enumerate((w0_ref, w1_ref, w2_ref)):
        term = lax.dot_general(
            w_ref[0], conv_ref[i], (((1,), (1,)), ((), ())), preferred_element_type=F32
        )
        total = term if total is None else total + term
    total = total.T
    if len(rest) > 1:
        total = total + rest[0][...].astype(F32)
    out_ref[...] = total.astype(BF16)


def input_grad(conv, weights, member, first, extent, depth, grad=None):
    rows, channels = conv.shape[1:]
    width = SPAN
    steps = extent // width
    start = first // width
    whole = depth // width
    in_specs = [pl.BlockSpec((3, rows, channels), lambda j, m: (0, 0, 0))]
    for i in range(3):
        in_specs.append(
            pl.BlockSpec(
                (1, width, channels), lambda j, m, i=i: (i, m[0] * whole + start + j, 0)
            )
        )
    operands = [conv, weights, weights, weights]
    if grad is not None:
        in_specs.append(pl.BlockSpec((rows, width), lambda j, m: (0, start + j)))
        operands.append(grad)
    return pl.pallas_call(
        input_grad_kernel,
        grid_spec=pltpu.PrefetchScalarGridSpec(
            num_scalar_prefetch=1,
            grid=(steps,),
            in_specs=in_specs,
            out_specs=pl.BlockSpec((rows, width), lambda j, m: (0, j)),
        ),
        out_shape=jax.ShapeDtypeStruct((rows, extent), BF16),
        compiler_params=params(("arbitrary",)),
        cost_estimate=cost(1, 1),
        name="input_grad",
    )(member, *operands)


def join(pieces, depth):
    rows = pieces[0][1].shape[0]

    def kernel(*refs):
        out_ref = refs[-1]
        for start in range(0, depth, SPAN):
            total = None
            for (first, piece), ref in zip(pieces, refs):
                if first <= start < first + piece.shape[1]:
                    term = ref[:, start - first : start - first + SPAN].astype(F32)
                    total = term if total is None else total + term
            out_ref[:, start : start + SPAN] = total.astype(BF16)

    return pl.pallas_call(
        kernel,
        out_shape=jax.ShapeDtypeStruct((rows, depth), BF16),
        compiler_params=pltpu.CompilerParams(vmem_limit_bytes=VMEM_LIMIT),
        cost_estimate=cost(0, 6 * rows * depth),
        name="join",
    )(*[piece for _, piece in pieces])


SPAN = 256
AWAY_CUTS = (8,)
OWN_CUTS = (4, 4)


def cuts_of(eighths, depth):
    step = depth // 8
    if step % SPAN:
        return [(0, depth)]
    first, spans = 0, []
    for count in eighths:
        spans.append((first, count * step))
        first += count * step
    return spans


def local(block_input, incoming, in_weight, short_taps, medium_taps, skip_weight):
    micro, length, depth = block_input.shape[1:]
    rows = micro * length
    members = lax.axis_size("tp")
    sections = lax.axis_size("section")
    me = lax.axis_index("tp")
    weights = jnp.transpose(in_weight[0], (1, 0, 2))
    x = block_input.reshape(rows, depth)
    grad = incoming.reshape(rows, depth)

    def owner(step):
        return jnp.full((1,), lax.rem(me + step, members), jnp.int32)

    from_member = [x]
    for k in range(1, members):
        pairs = [((m + k) % members, m) for m in range(members)]
        from_member.append(lax.ppermute(x, "tp", pairs))
    so_far = None
    for k in range(members - 1):
        so_far = project(from_member[k], weights, owner(k), so_far)
    first, second = toeplitz_pair(medium_taps[0])
    conv = mixer(
        from_member[-1], weights, owner(members - 1), so_far, first, second,
        short_taps[0], skip_weight, grad, micro,
    )
    pieces = []
    for k in list(range(1, members)) + [0]:
        pairs = [
            (s * members + m, (s - 1) % sections * members + (m + k) % members)
            for s in range(sections)
            for m in range(members)
        ]
        for first_column, extent in cuts_of(AWAY_CUTS if k else OWN_CUTS, depth):
            share = input_grad(
                conv, weights, owner(k), first_column, extent, depth, None if k else grad
            )
            pieces.append((first_column, lax.ppermute(share, ("section", "tp"), pairs)))
    return join(pieces, depth).reshape(block_input.shape)


def solution(mesh):
    in_specs = (
        P("section", None, None, "tp"),
        P("section", None, None, "tp"),
        P("section", None, None, "tp"),
        P("section", None, None, "tp"),
        P("section", None, "tp"),
        P("section", "tp"),
    )
    out_specs = P("section", None, None, "tp")
    return jax.shard_map(local, mesh=mesh, in_specs=in_specs, out_specs=out_specs, check_vma=False)
```

```python
import functools

import jax
import jax.numpy as jnp
from jax import lax
from jax.experimental import pallas as pl
from jax.experimental.pallas import tpu as pltpu
from jax.sharding import PartitionSpec as P

F32 = jnp.float32
BF16 = jnp.bfloat16
LANES = 128
MIB = 1024 * 1024
VMEM_LIMIT = 8 * MIB
SPAN = 256
AWAY_CUTS = (8,)
OWN_CUTS = (4, 4)

IN_VMEM = pl.BlockSpec(memory_space=pltpu.VMEM)
IN_SMEM = pl.BlockSpec(memory_space=pltpu.SMEM)
ANYWHERE = pl.BlockSpec(memory_space=pl.ANY)


def params():
    return pltpu.CompilerParams(vmem_limit_bytes=VMEM_LIMIT)


def cost(flops, moved):
    return pl.CostEstimate(flops=flops, bytes_accessed=moved, transcendentals=0)


def held(array):
    return pltpu.with_memory_space_constraint(array, pltpu.VMEM)


def load_kernel(
    me_ref, x_ref, w_ref, medium_ref, held_ref, so_far_ref, first_ref, second_ref,
    sums, matrices, turned_ref, own_sem, rest_sem, sums_sem, first_sem, second_sem,
    *, members, width, rest_rows
):
    rows, depth = x_ref.shape
    channels = w_ref.shape[2]
    length, groups = medium_ref.shape
    me = me_ref[0]
    own_row = pl.multiple_of(me * depth, depth)
    blocks = channels // width

    def own_copy(n):
        place = (
            n // blocks,
            pl.ds(own_row, depth),
            pl.ds(pl.multiple_of(n % blocks * width, width), width),
        )
        return pltpu.make_async_copy(w_ref.at[place], held_ref.at[place], own_sem.at[n])

    rest = []
    for k in range(1, members):
        row = pl.multiple_of(lax.rem(me + k, members) * depth, depth)
        for i in range(3):
            for part in range(depth // rest_rows):
                place = (i, pl.ds(pl.multiple_of(row + part * rest_rows, rest_rows), rest_rows))
                rest.append(
                    pltpu.make_async_copy(
                        w_ref.at[place], held_ref.at[place], rest_sem.at[len(rest)]
                    )
                )
    for n in range(3 * blocks):
        own_copy(n).start()
    for copy in rest:
        copy.start()

    places = lax.broadcasted_iota(jnp.int32, (length, length), 0)
    lags = lax.broadcasted_iota(jnp.int32, (length, length), 1)
    medium = medium_ref[...].astype(BF16)
    turns = (places == lags, (places + lags) % length == 0)
    for n, turn in enumerate(turns):
        turned_ref[n] = lax.dot_general(
            medium,
            jnp.where(turn, 1.0, 0.0).astype(BF16),
            (((0,), (0,)), ((), ())),
            preferred_element_type=F32,
        )
    step = 8
    keeps = (lags >= places, lags <= places)
    targets = (second_ref, first_ref)
    target_sems = (second_sem, first_sem)

    def matrix_copy(n, turn):
        slot = n % 2
        lanes = pl.ds(pl.multiple_of(n * step * length, step * length), step * length)
        return pltpu.make_async_copy(
            matrices.at[turn, slot], targets[turn].at[:, lanes], target_sems[turn].at[slot]
        )

    def matrix_step(n, carry):
        for turn in range(2):
            @pl.when(n >= 2)
            def _():
                matrix_copy(n - 2, turn).wait()

            lines = turned_ref[turn, pl.ds(pl.multiple_of(n * step, step), step), :]
            for g in range(step):
                base = jnp.broadcast_to(lines[g : g + 1], (length, length))
                rolled = pltpu.roll(base, 0, 1, stride=1, stride_axis=0)
                matrices[turn, n % 2, :, g * length : (g + 1) * length] = jnp.where(
                    keeps[turn], rolled, 0.0
                ).astype(BF16)
            matrix_copy(n, turn).start()
        return carry

    matrix_steps = groups // step
    lax.fori_loop(0, matrix_steps, matrix_step, 0)
    for n in range(max(matrix_steps - 2, 0), matrix_steps):
        for turn in range(2):
            matrix_copy(n, turn).wait()

    def sums_copy(n):
        slot = n % 2
        lanes = pl.ds(pl.multiple_of(n % blocks * width, width), width)
        return pltpu.make_async_copy(
            sums.at[slot], so_far_ref.at[n // blocks, :, lanes], sums_sem.at[slot]
        )

    def sums_step(n, carry):
        own_copy(n).wait()

        @pl.when(n >= 2)
        def _():
            sums_copy(n - 2).wait()

        lanes = pl.ds(pl.multiple_of(n % blocks * width, width), width)
        sums[n % 2] = jnp.dot(
            x_ref[...],
            held_ref[n // blocks, pl.ds(own_row, depth), lanes],
            preferred_element_type=F32,
        )
        sums_copy(n).start()
        return carry

    lax.fori_loop(0, 3 * blocks, sums_step, 0)
    for n in range(3 * blocks - 2, 3 * blocks):
        sums_copy(n).wait()
    for copy in rest:
        copy.wait()


def load(me, x, weights, medium, members):
    rows, depth = x.shape
    channels = weights.shape[2]
    length, groups = medium.shape
    width = min(512, channels)
    rest_rows = min(512, depth)
    matrix = jax.ShapeDtypeStruct((length, groups * length), BF16)
    return pl.pallas_call(
        functools.partial(load_kernel, members=members, width=width, rest_rows=rest_rows),
        in_specs=[IN_SMEM, IN_VMEM, ANYWHERE, IN_VMEM],
        out_specs=[IN_VMEM, ANYWHERE, ANYWHERE, ANYWHERE],
        out_shape=[
            pltpu.VMEM(weights.shape, BF16),
            jax.ShapeDtypeStruct((3, rows, channels), F32),
            matrix,
            matrix,
        ],
        scratch_shapes=[
            pltpu.VMEM((2, rows, width), F32),
            pltpu.VMEM((2, 2, length, 8 * length), BF16),
            pltpu.VMEM((2, groups, length), F32),
            pltpu.SemaphoreType.DMA((3 * channels // width,)),
            pltpu.SemaphoreType.DMA(((members - 1) * 3 * depth // rest_rows,)),
            pltpu.SemaphoreType.DMA((2,)),
            pltpu.SemaphoreType.DMA((2,)),
            pltpu.SemaphoreType.DMA((2,)),
        ],
        compiler_params=params(),
        cost_estimate=cost(6 * rows * depth * channels, 2 * weights.size),
        name="load",
    )(me, x, weights, medium)


def down(series, steps):
    moved = pltpu.roll(series, steps, 0)
    row = lax.broadcasted_iota(jnp.int32, (8, series.shape[1]), 0)
    return jnp.concatenate([jnp.where(row >= steps, moved[:8], 0.0), moved[8:]], axis=0)


def up(series, steps):
    length = series.shape[0]
    moved = pltpu.roll(series, length - steps, 0)
    row = lax.broadcasted_iota(jnp.int32, (8, series.shape[1]), 0)
    last = jnp.where(row < 8 - steps, moved[length - 8 :], 0.0)
    return jnp.concatenate([moved[: length - 8], last], axis=0)


def short_filter(series, taps, move):
    shifted = [series] + [move(series, steps) for steps in range(1, 4)]
    near = taps[0] * series
    far = None
    for lag in range(1, len(taps)):
        term = taps[lag] * shifted[lag % 4]
        if lag < 4:
            near = near + term
        else:
            far = term if far is None else far + term
    if far is None:
        return near
    return near + move(far, 4)


def group_masks(members, width):
    group = lax.broadcasted_iota(jnp.int32, (1, width), 1) % LANES // members
    return [jnp.where(group == g, 1.0, 0.0).astype(BF16) for g in range(LANES // members)]


def medium_filter(toeplitz, series, masks):
    rounded = series.astype(BF16)
    stacked = jnp.concatenate([rounded * mask for mask in masks], axis=0)
    return jnp.dot(toeplitz, stacked, preferred_element_type=F32)


def mixer_kernel(
    me_ref, w_ref, taps_ref, skip_ref, grad_ref, so_far_ref, first_ref, second_ref, *rest,
    members, micro, group, width
):
    x_refs = rest[: members - 1]
    out_ref, so_far, first, second, so_far_sem, first_sem, second_sem = rest[members - 1 :]
    rows = out_ref.shape[1]
    channels = out_ref.shape[2]
    length = rows // micro
    depth = x_refs[0].shape[1]
    reach = taps_ref.shape[0] * LANES // 3 // channels
    tiles = channels // LANES
    spread = LANES // group * length
    window = width // group * length
    blocks = channels // width
    me = me_ref[0]
    masks = group_masks(group, micro * LANES)

    def copies(n):
        slot = n % 2
        lanes = pl.ds(pl.multiple_of(n * width, width), width)
        wide = pl.ds(pl.multiple_of(n * window, window), window)
        return (
            pltpu.make_async_copy(
                so_far_ref.at[:, :, lanes], so_far.at[slot], so_far_sem.at[slot]
            ),
            pltpu.make_async_copy(first_ref.at[:, wide], first.at[slot], first_sem.at[slot]),
            pltpu.make_async_copy(second_ref.at[:, wide], second.at[slot], second_sem.at[slot]),
        )

    for copy in copies(0):
        copy.start()

    def step(n, carry):
        slot = n % 2

        @pl.when(n + 1 < blocks)
        def _():
            for copy in copies(n + 1):
                copy.start()

        for copy in copies(n):
            copy.wait()
        lanes_all = pl.ds(pl.multiple_of(n * width, width), width)
        projected = []
        for i in range(3):
            total = so_far[slot, i]
            for k, x_ref in enumerate(x_refs):
                row = pl.multiple_of(lax.rem(me + k + 1, members) * depth, depth)
                total = total + jnp.dot(
                    x_ref[...],
                    w_ref[i, pl.ds(row, depth), lanes_all],
                    preferred_element_type=F32,
                )
            projected.append(total)
        for tile in range(width // LANES):
            inner = slice(tile * LANES, (tile + 1) * LANES)
            lanes = pl.ds(pl.multiple_of(n * width + tile * LANES, LANES), LANES)
            line = n * (width // LANES) + tile
            taps = [
                [taps_ref[pl.ds((j * 3 + i) * tiles + line, 1), :] for j in range(reach)]
                for i in range(3)
            ]
            skip = skip_ref[0:1, lanes]
            places = slice(tile * spread, (tile + 1) * spread)
            query, key, value, upstream = [], [], [], []
            for b in range(micro):
                span = slice(b * length, (b + 1) * length)
                series = [short_filter(projected[i][span, inner], taps[i], down) for i in range(3)]
                query.append(series[0])
                key.append(series[1])
                value.append(series[2])
                upstream.append(grad_ref[span, lanes].astype(F32))
            product = [k * v for k, v in zip(key, value)]
            mixed = medium_filter(first[slot, :, places], jnp.concatenate(product, axis=1), masks)
            mixed_grad = [u * q for u, q in zip(upstream, query)]
            product_grad = medium_filter(
                second[slot, :, places], jnp.concatenate(mixed_grad, axis=1), masks
            )
            for b in range(micro):
                span = slice(b * length, (b + 1) * length)
                part = slice(b * LANES, (b + 1) * LANES)
                back = product_grad[:, part] + skip * mixed_grad[b]
                grads = [
                    upstream[b] * (mixed[:, part] + skip * product[b]),
                    back * value[b],
                    back * key[b],
                ]
                for i in range(3):
                    out_ref[i, span, lanes] = short_filter(grads[i], taps[i], up).astype(BF16)
        return carry

    lax.fori_loop(0, blocks, step, 0)


def mixer(me, weights, taps, skip, grad, so_far, first, second, others, micro):
    rows, depth = others[0].shape
    members = len(others) + 1
    channels = weights.shape[2]
    length = rows // micro
    groups = first.shape[1] // length
    group = channels // groups
    width = min(256, channels)
    window = width // group * length
    return pl.pallas_call(
        functools.partial(
            mixer_kernel, members=members, micro=micro, group=group, width=width
        ),
        in_specs=[IN_SMEM, IN_VMEM, IN_VMEM, IN_VMEM, IN_VMEM]
        + [ANYWHERE] * 3
        + [IN_VMEM] * len(others),
        out_specs=IN_VMEM,
        out_shape=pltpu.VMEM((3, rows, channels), BF16),
        scratch_shapes=[
            pltpu.VMEM((2, 3, rows, width), F32),
            pltpu.VMEM((2, length, window), BF16),
            pltpu.VMEM((2, length, window), BF16),
            pltpu.SemaphoreType.DMA((2,)),
            pltpu.SemaphoreType.DMA((2,)),
            pltpu.SemaphoreType.DMA((2,)),
        ],
        compiler_params=params(),
        cost_estimate=cost(6 * rows * depth * channels, 18 * rows * channels),
        name="mixer",
    )(me, held(weights), taps, skip, grad, so_far, first, second, *map(held, others))


def input_grad_kernel(member_ref, conv_ref, w_ref, *rest, first, depth, width):
    out_ref = rest[-1]
    start = member_ref[0] * depth + first
    for step in range(out_ref.shape[1] // width):
        place = slice(step * width, (step + 1) * width)
        row = pl.multiple_of(start + step * width, width)
        total = None
        for i in range(3):
            term = lax.dot_general(
                w_ref[i, pl.ds(row, width), :],
                conv_ref[i],
                (((1,), (1,)), ((), ())),
                preferred_element_type=F32,
            )
            total = term if total is None else total + term
        total = total.T
        if len(rest) > 1:
            total = total + rest[0][:, first + step * width : first + (step + 1) * width].astype(F32)
        out_ref[:, place] = total.astype(BF16)


def input_grad(conv, weights, member, first, extent, depth, grad=None):
    rows = conv.shape[1]
    operands = [conv, weights] + ([] if grad is None else [grad])
    return pl.pallas_call(
        functools.partial(input_grad_kernel, first=first, depth=depth, width=SPAN),
        in_specs=[IN_SMEM] + [IN_VMEM] * len(operands),
        out_specs=IN_VMEM,
        out_shape=jax.ShapeDtypeStruct((rows, extent), BF16),
        compiler_params=params(),
        cost_estimate=cost(1, 1),
        name="input_grad",
    )(member, held(conv), held(weights), *operands[2:])


def join(pieces, depth):
    rows = pieces[0][1].shape[0]

    def kernel(*refs):
        out_ref = refs[-1]
        for start in range(0, depth, SPAN):
            total = None
            for (first, piece), ref in zip(pieces, refs):
                if first <= start < first + piece.shape[1]:
                    term = ref[:, start - first : start - first + SPAN].astype(F32)
                    total = term if total is None else total + term
            out_ref[:, start : start + SPAN] = total.astype(BF16)

    return pl.pallas_call(
        kernel,
        out_shape=jax.ShapeDtypeStruct((rows, depth), BF16),
        compiler_params=params(),
        cost_estimate=cost(0, 6 * rows * depth),
        name="join",
    )(*[piece for _, piece in pieces])


def cuts_of(eighths, depth):
    step = depth // 8
    if step % SPAN:
        return [(0, depth)]
    first, spans = 0, []
    for count in eighths:
        spans.append((first, count * step))
        first += count * step
    return spans


def local(block_input, incoming, in_weight, short_taps, medium_taps, skip_weight):
    micro, length, depth = block_input.shape[1:]
    rows = micro * length
    members = lax.axis_size("tp")
    sections = lax.axis_size("section")
    me = lax.axis_index("tp")
    weights = jnp.transpose(in_weight[0], (1, 0, 2))
    x = block_input.reshape(rows, depth)
    grad = incoming.reshape(rows, depth)

    def owner(step):
        return jnp.full((1,), lax.rem(me + step, members), jnp.int32)

    others = []
    for k in range(1, members):
        pairs = [((m + k) % members, m) for m in range(members)]
        others.append(lax.ppermute(x, "tp", pairs))
    weights, so_far, first, second = load(owner(0), x, weights, medium_taps[0], members)
    conv = mixer(
        owner(0), weights, short_taps.reshape(-1, LANES), skip_weight, grad, so_far, first,
        second, others, micro,
    )
    pieces = []
    for k in list(range(1, members)) + [0]:
        pairs = [
            (s * members + m, (s - 1) % sections * members + (m + k) % members)
            for s in range(sections)
            for m in range(members)
        ]
        for first_column, extent in cuts_of(AWAY_CUTS if k else OWN_CUTS, depth):
            share = input_grad(
                conv, weights, owner(k), first_column, extent, depth, None if k else grad
            )
            pieces.append((first_column, lax.ppermute(share, ("section", "tp"), pairs)))
    return join(pieces, depth).reshape(block_input.shape)


def solution(mesh):
    in_specs = (
        P("section", None, None, "tp"),
        P("section", None, None, "tp"),
        P("section", None, None, "tp"),
        P("section", None, None, "tp"),
        P("section", None, "tp"),
        P("section", "tp"),
    )
    out_specs = P("section", None, None, "tp")
    return jax.shard_map(local, mesh=mesh, in_specs=in_specs, out_specs=out_specs, check_vma=False)
```

```python
import functools

import jax
import jax.numpy as jnp
from jax import lax
from jax.experimental import pallas as pl
from jax.experimental.pallas import tpu as pltpu
from jax.sharding import PartitionSpec as P

F32 = jnp.float32
BF16 = jnp.bfloat16
LANES = 128
MIB = 1024 * 1024
VMEM_LIMIT = 8 * MIB
SPAN = 256
AWAY_CUTS = (8,)
OWN_CUTS = (4, 4)

IN_VMEM = pl.BlockSpec(memory_space=pltpu.VMEM)
IN_SMEM = pl.BlockSpec(memory_space=pltpu.SMEM)
ANYWHERE = pl.BlockSpec(memory_space=pl.ANY)


def params(limit=VMEM_LIMIT):
    return pltpu.CompilerParams(vmem_limit_bytes=limit)


def cost(flops, moved):
    return pl.CostEstimate(flops=flops, bytes_accessed=moved, transcendentals=0)


def held(array):
    return pltpu.with_memory_space_constraint(array, pltpu.VMEM)


def load_kernel(
    me_ref, x_ref, w_ref, medium_ref, held_ref, so_far_ref, first_ref, second_ref,
    sums, matrices, turned_ref, own_sem, rest_sem, sums_sem, first_sem, second_sem,
    *, members, width, rest_rows
):
    rows, depth = x_ref.shape
    channels = w_ref.shape[2]
    length, groups = medium_ref.shape
    me = me_ref[0]
    own_row = pl.multiple_of(me * depth, depth)
    blocks = channels // width

    def own_copy(n):
        place = (
            n // blocks,
            pl.ds(own_row, depth),
            pl.ds(pl.multiple_of(n % blocks * width, width), width),
        )
        return pltpu.make_async_copy(w_ref.at[place], held_ref.at[place], own_sem.at[n])

    rest = []
    for k in range(1, members):
        row = pl.multiple_of(lax.rem(me + k, members) * depth, depth)
        for i in range(3):
            for part in range(depth // rest_rows):
                place = (i, pl.ds(pl.multiple_of(row + part * rest_rows, rest_rows), rest_rows))
                rest.append(
                    pltpu.make_async_copy(
                        w_ref.at[place], held_ref.at[place], rest_sem.at[len(rest)]
                    )
                )
    for n in range(3 * blocks):
        own_copy(n).start()
    for copy in rest:
        copy.start()

    places = lax.broadcasted_iota(jnp.int32, (length, length), 0)
    lags = lax.broadcasted_iota(jnp.int32, (length, length), 1)
    medium = medium_ref[...].astype(BF16)
    turns = (places == lags, (places + lags) % length == 0)
    for n, turn in enumerate(turns):
        turned_ref[n] = lax.dot_general(
            medium,
            jnp.where(turn, 1.0, 0.0).astype(BF16),
            (((0,), (0,)), ((), ())),
            preferred_element_type=F32,
        )
    step = 8
    keeps = (lags >= places, lags <= places)
    targets = (second_ref, first_ref)
    target_sems = (second_sem, first_sem)

    def matrix_copy(n, turn):
        slot = n % 2
        lanes = pl.ds(pl.multiple_of(n * step * length, step * length), step * length)
        return pltpu.make_async_copy(
            matrices.at[turn, slot], targets[turn].at[:, lanes], target_sems[turn].at[slot]
        )

    def matrix_step(n, carry):
        for turn in range(2):
            @pl.when(n >= 2)
            def _():
                matrix_copy(n - 2, turn).wait()

            lines = turned_ref[turn, pl.ds(pl.multiple_of(n * step, step), step), :]
            for g in range(step):
                base = jnp.broadcast_to(lines[g : g + 1], (length, length))
                rolled = pltpu.roll(base, 0, 1, stride=1, stride_axis=0)
                matrices[turn, n % 2, :, g * length : (g + 1) * length] = jnp.where(
                    keeps[turn], rolled, 0.0
                ).astype(BF16)
            matrix_copy(n, turn).start()
        return carry

    matrix_steps = groups // step
    lax.fori_loop(0, matrix_steps, matrix_step, 0)
    for n in range(max(matrix_steps - 2, 0), matrix_steps):
        for turn in range(2):
            matrix_copy(n, turn).wait()

    def sums_copy(n):
        slot = n % 2
        lanes = pl.ds(pl.multiple_of(n % blocks * width, width), width)
        return pltpu.make_async_copy(
            sums.at[slot], so_far_ref.at[n // blocks, :, lanes], sums_sem.at[slot]
        )

    def sums_step(n, carry):
        own_copy(n).wait()

        @pl.when(n >= 2)
        def _():
            sums_copy(n - 2).wait()

        lanes = pl.ds(pl.multiple_of(n % blocks * width, width), width)
        sums[n % 2] = jnp.dot(
            x_ref[...],
            held_ref[n // blocks, pl.ds(own_row, depth), lanes],
            preferred_element_type=F32,
        )
        sums_copy(n).start()
        return carry

    lax.fori_loop(0, 3 * blocks, sums_step, 0)
    for n in range(3 * blocks - 2, 3 * blocks):
        sums_copy(n).wait()
    for copy in rest:
        copy.wait()


def load(me, x, weights, medium, members):
    rows, depth = x.shape
    channels = weights.shape[2]
    length, groups = medium.shape
    width = min(512, channels)
    rest_rows = min(512, depth)
    matrix = jax.ShapeDtypeStruct((length, groups * length), BF16)
    return pl.pallas_call(
        functools.partial(load_kernel, members=members, width=width, rest_rows=rest_rows),
        in_specs=[IN_SMEM, IN_VMEM, ANYWHERE, IN_VMEM],
        out_specs=[IN_VMEM, ANYWHERE, ANYWHERE, ANYWHERE],
        out_shape=[
            pltpu.VMEM(weights.shape, BF16),
            jax.ShapeDtypeStruct((3, rows, channels), F32),
            matrix,
            matrix,
        ],
        scratch_shapes=[
            pltpu.VMEM((2, rows, width), F32),
            pltpu.VMEM((2, 2, length, 8 * length), BF16),
            pltpu.VMEM((2, groups, length), F32),
            pltpu.SemaphoreType.DMA((3 * channels // width,)),
            pltpu.SemaphoreType.DMA(((members - 1) * 3 * depth // rest_rows,)),
            pltpu.SemaphoreType.DMA((2,)),
            pltpu.SemaphoreType.DMA((2,)),
            pltpu.SemaphoreType.DMA((2,)),
        ],
        compiler_params=params(),
        cost_estimate=cost(6 * rows * depth * channels, 2 * weights.size),
        name="load",
    )(me, x, weights, medium)


STRIP = 8
NEAR = 4


def strip_filter(strip, taps, passed, back):
    row = lax.broadcasted_iota(jnp.int32, strip.shape, 0)

    def moved(series, lag):
        return pltpu.roll(series, STRIP - lag if back else lag, 0)

    def joined(own, before, lag):
        outside = row >= STRIP - lag if back else row < lag
        return jnp.where(outside, 0.0 if before is None else before, own)

    turned = [moved(strip, lag) for lag in range(1, NEAR)]
    lagged = [strip] + [
        joined(own, None if passed is None else passed[0][n], n + 1)
        for n, own in enumerate(turned)
    ]
    near, far = (
        functools.reduce(
            lambda total, term: total + term,
            [tap * series for tap, series in zip(span, lagged)],
        )
        for span in (taps[:NEAR], taps[NEAR:])
    )
    far = moved(far, NEAR)
    result = near + joined(far, None if passed is None else passed[1], NEAR)
    return result, (turned, far)


def group_masks(members, width):
    group = lax.broadcasted_iota(jnp.int32, (1, width), 1) % LANES // members
    return [jnp.where(group == g, 1.0, 0.0).astype(BF16) for g in range(LANES // members)]


def mixer_kernel(
    me_ref, w_ref, taps_ref, skip_ref, grad_ref, so_far_ref, first_ref, second_ref, *rest,
    members, micro, group, width
):
    x_refs = rest[: members - 1]
    (
        out_ref, so_far, first, second, coming, projected, keys, values, mixed_grads, rounded,
        so_far_sem, first_sem, second_sem,
    ) = rest[members - 1 :]
    rows = out_ref.shape[1]
    channels = out_ref.shape[2]
    length = rows // micro
    depth = x_refs[0].shape[1]
    reach = taps_ref.shape[0] * LANES // 3 // channels
    tiles = channels // LANES
    spread = LANES // group * length
    window = width // group * length
    blocks = channels // width
    pairs = length // (2 * STRIP)
    me = me_ref[0]
    masks = group_masks(group, micro * LANES)

    def sums_copy(n):
        lanes = pl.ds(pl.multiple_of(n * width, width), width)
        return pltpu.make_async_copy(so_far_ref.at[:, :, lanes], so_far, so_far_sem)

    def matrix_copies(n):
        slot = n % 2
        wide = pl.ds(pl.multiple_of(n * window, window), window)
        return (
            pltpu.make_async_copy(first_ref.at[:, wide], first.at[slot], first_sem.at[slot]),
            pltpu.make_async_copy(second_ref.at[:, wide], second.at[slot], second_sem.at[slot]),
        )

    def project(n, i):
        lanes = pl.ds(pl.multiple_of(n * width, width), width)
        total = None
        for k, x_ref in enumerate(x_refs):
            row = pl.multiple_of(lax.rem(me + k + 1, members) * depth, depth)
            term = jnp.dot(
                x_ref[...], w_ref[i, pl.ds(row, depth), lanes], preferred_element_type=F32
            )
            total = term if total is None else total + term
        coming[i] = total

    def take_over():
        for i in range(3):
            projected[i] = coming[i] + so_far[i]

    def forward(n, tile, taps):
        inner = slice(tile * LANES, (tile + 1) * LANES)
        lanes = pl.ds(pl.multiple_of(n * width + tile * LANES, LANES), LANES)
        for b in range(micro):
            place = slice(b * LANES, (b + 1) * LANES)
            passed = [None] * 3
            for pair in range(pairs):
                start = b * length + pair * 2 * STRIP
                upstream = grad_ref[start : start + 2 * STRIP, lanes].astype(F32)
                products, backs = [], []
                for half in range(2):
                    span = slice(start + half * STRIP, start + (half + 1) * STRIP)
                    series = [None] * 3
                    for i in range(3):
                        series[i], passed[i] = strip_filter(
                            projected[i, span, inner], taps[i], passed[i], False
                        )
                    query, key, value = series
                    mixed_grad = upstream[half * STRIP : (half + 1) * STRIP] * query
                    keys[span, inner] = key
                    values[span, inner] = value
                    mixed_grads[span, inner] = mixed_grad
                    products.append(key * value)
                    backs.append(mixed_grad)
                held_rows = slice(pair * 2 * STRIP, (pair + 1) * 2 * STRIP)
                rounded[0, tile, held_rows, place] = jnp.concatenate(products, axis=0).astype(BF16)
                rounded[1, tile, held_rows, place] = jnp.concatenate(backs, axis=0).astype(BF16)

    def medium(n, tile):
        places = slice(tile * spread, (tile + 1) * spread)
        return [
            jnp.dot(
                matrix[n % 2, :, places],
                jnp.concatenate([rounded[turn, tile] * mask for mask in masks], axis=0),
                preferred_element_type=F32,
            )
            for turn, matrix in enumerate((first, second))
        ]

    def backward(n, tile, taps, mixed, product_grad):
        inner = slice(tile * LANES, (tile + 1) * LANES)
        lanes = pl.ds(pl.multiple_of(n * width + tile * LANES, LANES), LANES)
        skip = jnp.broadcast_to(skip_ref[0:1, lanes], (STRIP, LANES))
        for b in range(micro):
            place = slice(b * LANES, (b + 1) * LANES)
            passed = [None] * 3
            for pair in reversed(range(pairs)):
                start = b * length + pair * 2 * STRIP
                upstream = grad_ref[start : start + 2 * STRIP, lanes].astype(F32)
                results = [[None] * 2 for _ in range(3)]
                for half in (1, 0):
                    span = slice(start + half * STRIP, start + (half + 1) * STRIP)
                    own = slice(
                        pair * 2 * STRIP + half * STRIP, pair * 2 * STRIP + (half + 1) * STRIP
                    )
                    key, value = keys[span, inner], values[span, inner]
                    back = product_grad[own, place] + skip * mixed_grads[span, inner]
                    grads = [
                        upstream[half * STRIP : (half + 1) * STRIP]
                        * (mixed[own, place] + skip * (key * value)),
                        back * value,
                        back * key,
                    ]
                    for i in range(3):
                        results[i][half], passed[i] = strip_filter(
                            grads[i], taps[i], passed[i], True
                        )
                for i in range(3):
                    out_ref[i, start : start + 2 * STRIP, lanes] = jnp.concatenate(
                        results[i], axis=0
                    ).astype(BF16)

    sums_copy(0).start()
    for copy in matrix_copies(0):
        copy.start()
    for i in range(3):
        project(0, i)
    sums_copy(0).wait()
    take_over()

    def step(n, carry):
        following = jnp.minimum(n + 1, blocks - 1)

        @pl.when(n + 1 < blocks)
        def _():
            for copy in matrix_copies(n + 1):
                copy.start()
            sums_copy(n + 1).start()

        for copy in matrix_copies(n):
            copy.wait()
        taps = []
        for tile in range(width // LANES):
            line = n * (width // LANES) + tile
            taps.append([
                [
                    jnp.broadcast_to(
                        taps_ref[pl.ds((j * 3 + i) * tiles + line, 1), :], (STRIP, LANES)
                    )
                    for j in range(reach)
                ]
                for i in range(3)
            ])
        work = [functools.partial(project, following, i) for i in range(3)]
        for tile in range(width // LANES):
            if work:
                work.pop(0)()
            forward(n, tile, taps[tile])
        for tile in range(width // LANES):
            if work:
                work.pop(0)()
            backward(n, tile, taps[tile], *medium(n, tile))
        for late in work:
            late()

        @pl.when(n + 1 < blocks)
        def _():
            sums_copy(n + 1).wait()
            take_over()

        return carry

    lax.fori_loop(0, blocks, step, 0)


def mixer(me, weights, taps, skip, grad, so_far, first, second, others, micro):
    rows, depth = others[0].shape
    members = len(others) + 1
    channels = weights.shape[2]
    length = rows // micro
    groups = first.shape[1] // length
    group = channels // groups
    width = min(256, channels)
    window = width // group * length
    return pl.pallas_call(
        functools.partial(
            mixer_kernel, members=members, micro=micro, group=group, width=width
        ),
        in_specs=[IN_SMEM, IN_VMEM, IN_VMEM, IN_VMEM, IN_VMEM]
        + [ANYWHERE] * 3
        + [IN_VMEM] * len(others),
        out_specs=IN_VMEM,
        out_shape=pltpu.VMEM((3, rows, channels), BF16),
        scratch_shapes=[
            pltpu.VMEM((3, rows, width), F32),
            pltpu.VMEM((2, length, window), BF16),
            pltpu.VMEM((2, length, window), BF16),
            pltpu.VMEM((3, rows, width), F32),
            pltpu.VMEM((3, rows, width), F32),
            pltpu.VMEM((rows, width), F32),
            pltpu.VMEM((rows, width), F32),
            pltpu.VMEM((rows, width), F32),
            pltpu.VMEM((2, width // LANES, length, micro * LANES), BF16),
            pltpu.SemaphoreType.DMA,
            pltpu.SemaphoreType.DMA((2,)),
            pltpu.SemaphoreType.DMA((2,)),
        ],
        compiler_params=params(10 * MIB),
        cost_estimate=cost(6 * rows * depth * channels, 18 * rows * channels),
        name="mixer",
    )(me, held(weights), taps, skip, grad, so_far, first, second, *map(held, others))


def input_grad_kernel(member_ref, conv_ref, w_ref, *rest, first, depth, width):
    out_ref = rest[-1]
    start = member_ref[0] * depth + first
    for step in range(out_ref.shape[1] // width):
        place = slice(step * width, (step + 1) * width)
        row = pl.multiple_of(start + step * width, width)
        total = None
        for i in range(3):
            term = lax.dot_general(
                w_ref[i, pl.ds(row, width), :],
                conv_ref[i],
                (((1,), (1,)), ((), ())),
                preferred_element_type=F32,
            )
            total = term if total is None else total + term
        total = total.T
        if len(rest) > 1:
            total = total + rest[0][:, first + step * width : first + (step + 1) * width].astype(F32)
        out_ref[:, place] = total.astype(BF16)


def input_grad(conv, weights, member, first, extent, depth, grad=None):
    rows = conv.shape[1]
    operands = [conv, weights] + ([] if grad is None else [grad])
    return pl.pallas_call(
        functools.partial(input_grad_kernel, first=first, depth=depth, width=SPAN),
        in_specs=[IN_SMEM] + [IN_VMEM] * len(operands),
        out_specs=IN_VMEM,
        out_shape=jax.ShapeDtypeStruct((rows, extent), BF16),
        compiler_params=params(),
        cost_estimate=cost(1, 1),
        name="input_grad",
    )(member, held(conv), held(weights), *operands[2:])


def join(pieces, depth):
    rows = pieces[0][1].shape[0]

    def kernel(*refs):
        out_ref = refs[-1]
        for start in range(0, depth, SPAN):
            total = None
            for (first, piece), ref in zip(pieces, refs):
                if first <= start < first + piece.shape[1]:
                    term = ref[:, start - first : start - first + SPAN].astype(F32)
                    total = term if total is None else total + term
            out_ref[:, start : start + SPAN] = total.astype(BF16)

    return pl.pallas_call(
        kernel,
        out_shape=jax.ShapeDtypeStruct((rows, depth), BF16),
        compiler_params=params(),
        cost_estimate=cost(0, 6 * rows * depth),
        name="join",
    )(*[piece for _, piece in pieces])


def cuts_of(eighths, depth):
    step = depth // 8
    if step % SPAN:
        return [(0, depth)]
    first, spans = 0, []
    for count in eighths:
        spans.append((first, count * step))
        first += count * step
    return spans


def local(block_input, incoming, in_weight, short_taps, medium_taps, skip_weight):
    micro, length, depth = block_input.shape[1:]
    rows = micro * length
    members = lax.axis_size("tp")
    sections = lax.axis_size("section")
    me = lax.axis_index("tp")
    weights = jnp.transpose(in_weight[0], (1, 0, 2))
    x = block_input.reshape(rows, depth)
    grad = incoming.reshape(rows, depth)

    def owner(step):
        return jnp.full((1,), lax.rem(me + step, members), jnp.int32)

    others = []
    for k in range(1, members):
        pairs = [((m + k) % members, m) for m in range(members)]
        others.append(lax.ppermute(x, "tp", pairs))
    weights, so_far, first, second = load(owner(0), x, weights, medium_taps[0], members)
    conv = mixer(
        owner(0), weights, short_taps.reshape(-1, LANES), skip_weight, grad, so_far, first,
        second, others, micro,
    )
    pieces = []
    for k in list(range(1, members)) + [0]:
        pairs = [
            (s * members + m, (s - 1) % sections * members + (m + k) % members)
            for s in range(sections)
            for m in range(members)
        ]
        for first_column, extent in cuts_of(AWAY_CUTS if k else OWN_CUTS, depth):
            share = input_grad(
                conv, weights, owner(k), first_column, extent, depth, None if k else grad
            )
            pieces.append((first_column, lax.ppermute(share, ("section", "tp"), pairs)))
    return join(pieces, depth).reshape(block_input.shape)


def solution(mesh):
    in_specs = (
        P("section", None, None, "tp"),
        P("section", None, None, "tp"),
        P("section", None, None, "tp"),
        P("section", None, None, "tp"),
        P("section", None, "tp"),
        P("section", "tp"),
    )
    out_specs = P("section", None, None, "tp")
    return jax.shard_map(local, mesh=mesh, in_specs=in_specs, out_specs=out_specs, check_vma=False)
```

```python
import functools
import math

import jax
import jax.numpy as jnp
from jax import lax
from jax.experimental import pallas as pl
from jax.experimental.pallas import tpu as pltpu
from jax.sharding import PartitionSpec as P

F32 = jnp.float32
BF16 = jnp.bfloat16
LANES = 128
MIB = 1024 * 1024
VMEM_LIMIT = 8 * MIB
SPAN = 256
SHARE_CUTS = (6, 2)
AWAY_CUTS = (8,)
OWN_CUTS = (4, 4)

IN_VMEM = pl.BlockSpec(memory_space=pltpu.VMEM)
IN_SMEM = pl.BlockSpec(memory_space=pltpu.SMEM)
ANYWHERE = pl.BlockSpec(memory_space=pl.ANY)


def params():
    return pltpu.CompilerParams(vmem_limit_bytes=VMEM_LIMIT)


def cost(flops, moved):
    return pl.CostEstimate(flops=flops, bytes_accessed=moved, transcendentals=0)


def held(array):
    return pltpu.with_memory_space_constraint(array, pltpu.VMEM)


def load_kernel(
    me_ref, x_ref, w_ref, medium_ref, held_ref, so_far_ref, first_ref, second_ref,
    sums, matrices, turned_ref, own_sem, rest_sem, sums_sem, first_sem, second_sem,
    *, members, width, rest_rows
):
    rows, depth = x_ref.shape
    channels = w_ref.shape[2]
    length, groups = medium_ref.shape
    me = me_ref[0]
    own_row = pl.multiple_of(me * depth, depth)
    blocks = channels // width

    def own_copy(n):
        place = (
            n // blocks,
            pl.ds(own_row, depth),
            pl.ds(pl.multiple_of(n % blocks * width, width), width),
        )
        return pltpu.make_async_copy(w_ref.at[place], held_ref.at[place], own_sem.at[n])

    rest = []
    for k in range(1, members):
        row = pl.multiple_of(lax.rem(me + k, members) * depth, depth)
        for i in range(3):
            for part in range(depth // rest_rows):
                place = (i, pl.ds(pl.multiple_of(row + part * rest_rows, rest_rows), rest_rows))
                rest.append(
                    pltpu.make_async_copy(
                        w_ref.at[place], held_ref.at[place], rest_sem.at[len(rest)]
                    )
                )
    for n in range(3 * blocks):
        own_copy(n).start()
    for copy in rest:
        copy.start()

    places = lax.broadcasted_iota(jnp.int32, (length, length), 0)
    lags = lax.broadcasted_iota(jnp.int32, (length, length), 1)
    medium = medium_ref[...].astype(BF16)
    turns = (places == lags, (places + lags) % length == 0)
    for n, turn in enumerate(turns):
        turned_ref[n] = lax.dot_general(
            medium,
            jnp.where(turn, 1.0, 0.0).astype(BF16),
            (((0,), (0,)), ((), ())),
            preferred_element_type=F32,
        )
    step = 8
    keeps = (lags >= places, lags <= places)
    targets = (second_ref, first_ref)
    target_sems = (second_sem, first_sem)

    def matrix_copy(n, turn):
        slot = n % 2
        lanes = pl.ds(pl.multiple_of(n * step * length, step * length), step * length)
        return pltpu.make_async_copy(
            matrices.at[turn, slot], targets[turn].at[:, lanes], target_sems[turn].at[slot]
        )

    def matrix_step(n, carry):
        for turn in range(2):
            @pl.when(n >= 2)
            def _():
                matrix_copy(n - 2, turn).wait()

            lines = turned_ref[turn, pl.ds(pl.multiple_of(n * step, step), step), :]
            for g in range(step):
                base = jnp.broadcast_to(lines[g : g + 1], (length, length))
                rolled = pltpu.roll(base, 0, 1, stride=1, stride_axis=0)
                matrices[turn, n % 2, :, g * length : (g + 1) * length] = jnp.where(
                    keeps[turn], rolled, 0.0
                ).astype(BF16)
            matrix_copy(n, turn).start()
        return carry

    matrix_steps = groups // step
    lax.fori_loop(0, matrix_steps, matrix_step, 0)
    for n in range(max(matrix_steps - 2, 0), matrix_steps):
        for turn in range(2):
            matrix_copy(n, turn).wait()

    def sums_copy(n):
        slot = n % 2
        lanes = pl.ds(pl.multiple_of(n % blocks * width, width), width)
        return pltpu.make_async_copy(
            sums.at[slot], so_far_ref.at[n // blocks, :, lanes], sums_sem.at[slot]
        )

    def sums_step(n, carry):
        own_copy(n).wait()

        @pl.when(n >= 2)
        def _():
            sums_copy(n - 2).wait()

        lanes = pl.ds(pl.multiple_of(n % blocks * width, width), width)
        sums[n % 2] = jnp.dot(
            x_ref[...],
            held_ref[n // blocks, pl.ds(own_row, depth), lanes],
            preferred_element_type=F32,
        )
        sums_copy(n).start()
        return carry

    lax.fori_loop(0, 3 * blocks, sums_step, 0)
    for n in range(3 * blocks - 2, 3 * blocks):
        sums_copy(n).wait()
    for copy in rest:
        copy.wait()


def load(me, x, weights, medium, members):
    rows, depth = x.shape
    channels = weights.shape[2]
    length, groups = medium.shape
    width = min(512, channels)
    rest_rows = min(512, depth)
    matrix = jax.ShapeDtypeStruct((length, groups * length), BF16)
    return pl.pallas_call(
        functools.partial(load_kernel, members=members, width=width, rest_rows=rest_rows),
        in_specs=[IN_SMEM, IN_VMEM, ANYWHERE, IN_VMEM],
        out_specs=[IN_VMEM, ANYWHERE, ANYWHERE, ANYWHERE],
        out_shape=[
            pltpu.VMEM(weights.shape, BF16),
            jax.ShapeDtypeStruct((3, rows, channels), F32),
            matrix,
            matrix,
        ],
        scratch_shapes=[
            pltpu.VMEM((2, rows, width), F32),
            pltpu.VMEM((2, 2, length, 8 * length), BF16),
            pltpu.VMEM((2, groups, length), F32),
            pltpu.SemaphoreType.DMA((3 * channels // width,)),
            pltpu.SemaphoreType.DMA(((members - 1) * 3 * depth // rest_rows,)),
            pltpu.SemaphoreType.DMA((2,)),
            pltpu.SemaphoreType.DMA((2,)),
            pltpu.SemaphoreType.DMA((2,)),
        ],
        compiler_params=params(),
        cost_estimate=cost(6 * rows * depth * channels, 2 * weights.size),
        name="load",
    )(me, x, weights, medium)


def project_kernel(
    member_ref, x_ref, w_ref, sums_ref, out_ref, before, after, before_sem, after_sem,
    *, depth, first, width
):
    rows, extent = x_ref.shape
    blocks = w_ref.shape[2] // width
    row = pl.multiple_of(member_ref[0] * depth + first, math.gcd(depth, first))

    def lanes(n):
        return pl.ds(pl.multiple_of(n % blocks * width, width), width)

    def before_copy(n):
        source = sums_ref.at[n // blocks, :, lanes(n)]
        return pltpu.make_async_copy(source, before.at[n % 2], before_sem.at[n % 2])

    def after_copy(n):
        target = out_ref.at[n // blocks, :, lanes(n)]
        return pltpu.make_async_copy(after.at[n % 2], target, after_sem.at[n % 2])

    before_copy(0).start()

    def step(n, carry):
        @pl.when(n + 1 < 3 * blocks)
        def _():
            before_copy(n + 1).start()

        @pl.when(n >= 2)
        def _():
            after_copy(n - 2).wait()

        before_copy(n).wait()
        after[n % 2] = before[n % 2] + jnp.dot(
            x_ref[...],
            w_ref[n // blocks, pl.ds(row, extent), lanes(n)],
            preferred_element_type=F32,
        )
        after_copy(n).start()
        return carry

    lax.fori_loop(0, 3 * blocks, step, 0)
    for n in range(3 * blocks - 2, 3 * blocks):
        after_copy(n).wait()


def project(member, x, first, depth, weights, sums):
    rows, extent = x.shape
    channels = weights.shape[2]
    width = min(512, channels)
    return pl.pallas_call(
        functools.partial(project_kernel, depth=depth, first=first, width=width),
        in_specs=[IN_SMEM, IN_VMEM, IN_VMEM, ANYWHERE],
        out_specs=ANYWHERE,
        out_shape=jax.ShapeDtypeStruct(sums.shape, F32),
        scratch_shapes=[
            pltpu.VMEM((2, rows, width), F32),
            pltpu.VMEM((2, rows, width), F32),
            pltpu.SemaphoreType.DMA((2,)),
            pltpu.SemaphoreType.DMA((2,)),
        ],
        compiler_params=params(),
        cost_estimate=cost(6 * rows * extent * channels, 24 * rows * channels),
        name="project",
    )(member, held(x), held(weights), sums)


STRIP = 8
NEAR = 4


def strip_filter(strip, taps, passed, back):
    row = lax.broadcasted_iota(jnp.int32, strip.shape, 0)

    def moved(series, lag):
        return pltpu.roll(series, STRIP - lag if back else lag, 0)

    def joined(own, before, lag):
        outside = row >= STRIP - lag if back else row < lag
        return jnp.where(outside, 0.0 if before is None else before, own)

    turned = [moved(strip, lag) for lag in range(1, NEAR)]
    lagged = [strip] + [
        joined(own, None if passed is None else passed[0][n], n + 1)
        for n, own in enumerate(turned)
    ]
    near, far = (
        functools.reduce(
            lambda total, term: total + term,
            [tap * series for tap, series in zip(span, lagged)],
        )
        for span in (taps[:NEAR], taps[NEAR:])
    )
    far = moved(far, NEAR)
    result = near + joined(far, None if passed is None else passed[1], NEAR)
    return result, (turned, far)


def group_masks(members, width):
    group = lax.broadcasted_iota(jnp.int32, (1, width), 1) % LANES // members
    return [jnp.where(group == g, 1.0, 0.0).astype(BF16) for g in range(LANES // members)]


def mixer_kernel(
    w_ref, taps_ref, skip_ref, grad_ref, sums_ref, first_ref, second_ref, out_ref,
    projected, first, second, keys, values, mixed_grads, rounded,
    sums_sem, first_sem, second_sem, *, micro, group, width
):
    del w_ref
    rows = out_ref.shape[1]
    channels = out_ref.shape[2]
    length = rows // micro
    reach = taps_ref.shape[0] * LANES // 3 // channels
    tiles = channels // LANES
    spread = LANES // group * length
    window = width // group * length
    blocks = channels // width
    pairs = length // (2 * STRIP)
    masks = group_masks(group, micro * LANES)

    def copies(n):
        slot = n % 2
        lanes = pl.ds(pl.multiple_of(n * width, width), width)
        wide = pl.ds(pl.multiple_of(n * window, window), window)
        return (
            pltpu.make_async_copy(
                sums_ref.at[:, :, lanes], projected.at[slot], sums_sem.at[slot]
            ),
            pltpu.make_async_copy(first_ref.at[:, wide], first.at[slot], first_sem.at[slot]),
            pltpu.make_async_copy(second_ref.at[:, wide], second.at[slot], second_sem.at[slot]),
        )

    def forward(n, tile, taps):
        inner = slice(tile * LANES, (tile + 1) * LANES)
        lanes = pl.ds(pl.multiple_of(n * width + tile * LANES, LANES), LANES)
        for b in range(micro):
            place = slice(b * LANES, (b + 1) * LANES)
            passed = [None] * 3
            for pair in range(pairs):
                start = b * length + pair * 2 * STRIP
                upstream = grad_ref[start : start + 2 * STRIP, lanes].astype(F32)
                products, backs = [], []
                for half in range(2):
                    span = slice(start + half * STRIP, start + (half + 1) * STRIP)
                    series = [None] * 3
                    for i in range(3):
                        series[i], passed[i] = strip_filter(
                            projected[n % 2, i, span, inner], taps[i], passed[i], False
                        )
                    query, key, value = series
                    mixed_grad = upstream[half * STRIP : (half + 1) * STRIP] * query
                    keys[span, inner] = key
                    values[span, inner] = value
                    mixed_grads[span, inner] = mixed_grad
                    products.append(key * value)
                    backs.append(mixed_grad)
                held_rows = slice(pair * 2 * STRIP, (pair + 1) * 2 * STRIP)
                rounded[0, tile, held_rows, place] = jnp.concatenate(products, axis=0).astype(BF16)
                rounded[1, tile, held_rows, place] = jnp.concatenate(backs, axis=0).astype(BF16)

    def medium(n, tile):
        places = slice(tile * spread, (tile + 1) * spread)
        return [
            jnp.dot(
                matrix[n % 2, :, places],
                jnp.concatenate([rounded[turn, tile] * mask for mask in masks], axis=0),
                preferred_element_type=F32,
            )
            for turn, matrix in enumerate((first, second))
        ]

    def backward(n, tile, taps, mixed, product_grad):
        inner = slice(tile * LANES, (tile + 1) * LANES)
        lanes = pl.ds(pl.multiple_of(n * width + tile * LANES, LANES), LANES)
        skip = jnp.broadcast_to(skip_ref[0:1, lanes], (STRIP, LANES))
        for b in range(micro):
            place = slice(b * LANES, (b + 1) * LANES)
            passed = [None] * 3
            for pair in reversed(range(pairs)):
                start = b * length + pair * 2 * STRIP
                upstream = grad_ref[start : start + 2 * STRIP, lanes].astype(F32)
                results = [[None] * 2 for _ in range(3)]
                for half in (1, 0):
                    span = slice(start + half * STRIP, start + (half + 1) * STRIP)
                    own = slice(
                        pair * 2 * STRIP + half * STRIP, pair * 2 * STRIP + (half + 1) * STRIP
                    )
                    key, value = keys[span, inner], values[span, inner]
                    back = product_grad[own, place] + skip * mixed_grads[span, inner]
                    grads = [
                        upstream[half * STRIP : (half + 1) * STRIP]
                        * (mixed[own, place] + skip * (key * value)),
                        back * value,
                        back * key,
                    ]
                    for i in range(3):
                        results[i][half], passed[i] = strip_filter(
                            grads[i], taps[i], passed[i], True
                        )
                for i in range(3):
                    out_ref[i, start : start + 2 * STRIP, lanes] = jnp.concatenate(
                        results[i], axis=0
                    ).astype(BF16)

    for copy in copies(0):
        copy.start()

    def step(n, carry):
        @pl.when(n + 1 < blocks)
        def _():
            for copy in copies(n + 1):
                copy.start()

        for copy in copies(n):
            copy.wait()
        taps = []
        for tile in range(width // LANES):
            line = n * (width // LANES) + tile
            taps.append([
                [
                    jnp.broadcast_to(
                        taps_ref[pl.ds((j * 3 + i) * tiles + line, 1), :], (STRIP, LANES)
                    )
                    for j in range(reach)
                ]
                for i in range(3)
            ])
        for tile in range(width // LANES):
            forward(n, tile, taps[tile])
        for tile in range(width // LANES):
            backward(n, tile, taps[tile], *medium(n, tile))
        return carry

    lax.fori_loop(0, blocks, step, 0)


def mixer(weights, taps, skip, grad, sums, first, second, micro):
    rows, channels = sums.shape[1:]
    length = rows // micro
    groups = first.shape[1] // length
    group = channels // groups
    width = min(256, channels)
    window = width // group * length
    return pl.pallas_call(
        functools.partial(mixer_kernel, micro=micro, group=group, width=width),
        in_specs=[IN_VMEM] * 4 + [ANYWHERE] * 3,
        out_specs=IN_VMEM,
        out_shape=pltpu.VMEM((3, rows, channels), BF16),
        scratch_shapes=[
            pltpu.VMEM((2, 3, rows, width), F32),
            pltpu.VMEM((2, length, window), BF16),
            pltpu.VMEM((2, length, window), BF16),
            pltpu.VMEM((rows, width), F32),
            pltpu.VMEM((rows, width), F32),
            pltpu.VMEM((rows, width), F32),
            pltpu.VMEM((2, width // LANES, length, micro * LANES), BF16),
            pltpu.SemaphoreType.DMA((2,)),
            pltpu.SemaphoreType.DMA((2,)),
            pltpu.SemaphoreType.DMA((2,)),
        ],
        compiler_params=params(),
        cost_estimate=cost(0, 18 * rows * channels),
        name="mixer",
    )(held(weights), taps, skip, grad, sums, first, second)


def input_grad_kernel(member_ref, conv_ref, w_ref, *rest, first, depth, width):
    out_ref = rest[-1]
    start = member_ref[0] * depth + first
    for step in range(out_ref.shape[1] // width):
        place = slice(step * width, (step + 1) * width)
        row = pl.multiple_of(start + step * width, width)
        total = None
        for i in range(3):
            term = lax.dot_general(
                w_ref[i, pl.ds(row, width), :],
                conv_ref[i],
                (((1,), (1,)), ((), ())),
                preferred_element_type=F32,
            )
            total = term if total is None else total + term
        total = total.T
        if len(rest) > 1:
            total = total + rest[0][:, first + step * width : first + (step + 1) * width].astype(F32)
        out_ref[:, place] = total.astype(BF16)


def input_grad(conv, weights, member, first, extent, depth, grad=None):
    rows = conv.shape[1]
    operands = [conv, weights] + ([] if grad is None else [grad])
    return pl.pallas_call(
        functools.partial(input_grad_kernel, first=first, depth=depth, width=SPAN),
        in_specs=[IN_SMEM] + [IN_VMEM] * len(operands),
        out_specs=IN_VMEM,
        out_shape=jax.ShapeDtypeStruct((rows, extent), BF16),
        compiler_params=params(),
        cost_estimate=cost(1, 1),
        name="input_grad",
    )(member, held(conv), held(weights), *operands[2:])


def join(pieces, depth):
    rows = pieces[0][1].shape[0]

    def kernel(*refs):
        out_ref = refs[-1]
        for start in range(0, depth, SPAN):
            total = None
            for (first, piece), ref in zip(pieces, refs):
                if first <= start < first + piece.shape[1]:
                    term = ref[:, start - first : start - first + SPAN].astype(F32)
                    total = term if total is None else total + term
            out_ref[:, start : start + SPAN] = total.astype(BF16)

    return pl.pallas_call(
        kernel,
        out_shape=jax.ShapeDtypeStruct((rows, depth), BF16),
        compiler_params=params(),
        cost_estimate=cost(0, 6 * rows * depth),
        name="join",
    )(*[piece for _, piece in pieces])


def cuts_of(eighths, depth):
    step = depth // 8
    if step % SPAN:
        return [(0, depth)]
    first, spans = 0, []
    for count in eighths:
        spans.append((first, count * step))
        first += count * step
    return spans


def local(block_input, incoming, in_weight, short_taps, medium_taps, skip_weight):
    micro, length, depth = block_input.shape[1:]
    rows = micro * length
    members = lax.axis_size("tp")
    sections = lax.axis_size("section")
    me = lax.axis_index("tp")
    weights = jnp.transpose(in_weight[0], (1, 0, 2))
    x = block_input.reshape(rows, depth)
    grad = incoming.reshape(rows, depth)

    def owner(step):
        return jnp.full((1,), lax.rem(me + step, members), jnp.int32)

    others = []
    for k in range(1, members):
        pairs = [((m + k) % members, m) for m in range(members)]
        for first_column, extent in cuts_of(SHARE_CUTS, depth):
            sent = x[:, first_column : first_column + extent]
            others.append((k, first_column, lax.ppermute(sent, "tp", pairs)))
    weights, sums, first, second = load(owner(0), x, weights, medium_taps[0], members)
    for k, first_column, share in others:
        sums = project(owner(k), share, first_column, depth, weights, sums)
    conv = mixer(
        weights, short_taps.reshape(-1, LANES), skip_weight, grad, sums, first, second, micro
    )
    pieces = []
    for k in list(range(1, members)) + [0]:
        pairs = [
            (s * members + m, (s - 1) % sections * members + (m + k) % members)
            for s in range(sections)
            for m in range(members)
        ]
        for first_column, extent in cuts_of(AWAY_CUTS if k else OWN_CUTS, depth):
            share = input_grad(
                conv, weights, owner(k), first_column, extent, depth, None if k else grad
            )
            pieces.append((first_column, lax.ppermute(share, ("section", "tp"), pairs)))
    return join(pieces, depth).reshape(block_input.shape)


def solution(mesh):
    in_specs = (
        P("section", None, None, "tp"),
        P("section", None, None, "tp"),
        P("section", None, None, "tp"),
        P("section", None, None, "tp"),
        P("section", None, "tp"),
        P("section", "tp"),
    )
    out_specs = P("section", None, None, "tp")
    return jax.shard_map(local, mesh=mesh, in_specs=in_specs, out_specs=out_specs, check_vma=False)
```

```python
import functools

import jax
import jax.numpy as jnp
from jax import lax
from jax.experimental import pallas as pl
from jax.experimental.pallas import tpu as pltpu
from jax.sharding import PartitionSpec as P

F32 = jnp.float32
BF16 = jnp.bfloat16
LANES = 128
MIB = 1024 * 1024
VMEM_LIMIT = 8 * MIB
SPAN = 256
AWAY_CUTS = (2, 6)
OWN_CUTS = (4, 4)

IN_VMEM = pl.BlockSpec(memory_space=pltpu.VMEM)
IN_SMEM = pl.BlockSpec(memory_space=pltpu.SMEM)
ANYWHERE = pl.BlockSpec(memory_space=pl.ANY)


def params():
    return pltpu.CompilerParams(vmem_limit_bytes=VMEM_LIMIT)


def cost(flops, moved):
    return pl.CostEstimate(flops=flops, bytes_accessed=moved, transcendentals=0)


def held(array):
    return pltpu.with_memory_space_constraint(array, pltpu.VMEM)


def load_kernel(
    me_ref, x_ref, w_ref, medium_ref, held_ref, so_far_ref, first_ref, second_ref,
    sums, matrices, turned_ref, own_sem, rest_sem, sums_sem, first_sem, second_sem,
    *, members, width, rest_rows
):
    rows, depth = x_ref.shape
    channels = w_ref.shape[2]
    length, groups = medium_ref.shape
    me = me_ref[0]
    own_row = pl.multiple_of(me * depth, depth)
    blocks = channels // width

    def own_copy(n):
        place = (
            n // blocks,
            pl.ds(own_row, depth),
            pl.ds(pl.multiple_of(n % blocks * width, width), width),
        )
        return pltpu.make_async_copy(w_ref.at[place], held_ref.at[place], own_sem.at[n])

    rest = []
    for k in range(1, members):
        row = pl.multiple_of(lax.rem(me + k, members) * depth, depth)
        for i in range(3):
            for part in range(depth // rest_rows):
                place = (i, pl.ds(pl.multiple_of(row + part * rest_rows, rest_rows), rest_rows))
                rest.append(
                    pltpu.make_async_copy(
                        w_ref.at[place], held_ref.at[place], rest_sem.at[len(rest)]
                    )
                )
    for n in range(3 * blocks):
        own_copy(n).start()
    for copy in rest:
        copy.start()

    places = lax.broadcasted_iota(jnp.int32, (length, length), 0)
    lags = lax.broadcasted_iota(jnp.int32, (length, length), 1)
    medium = medium_ref[...].astype(BF16)
    turns = (places == lags, (places + lags) % length == 0)
    for n, turn in enumerate(turns):
        turned_ref[n] = lax.dot_general(
            medium,
            jnp.where(turn, 1.0, 0.0).astype(BF16),
            (((0,), (0,)), ((), ())),
            preferred_element_type=F32,
        )
    step = 8
    keeps = (lags >= places, lags <= places)
    targets = (second_ref, first_ref)
    target_sems = (second_sem, first_sem)

    def matrix_copy(n, turn):
        slot = n % 2
        lanes = pl.ds(pl.multiple_of(n * step * length, step * length), step * length)
        return pltpu.make_async_copy(
            matrices.at[turn, slot], targets[turn].at[:, lanes], target_sems[turn].at[slot]
        )

    def matrix_step(n, carry):
        for turn in range(2):
            @pl.when(n >= 2)
            def _():
                matrix_copy(n - 2, turn).wait()

            lines = turned_ref[turn, pl.ds(pl.multiple_of(n * step, step), step), :]
            for g in range(step):
                base = jnp.broadcast_to(lines[g : g + 1], (length, length))
                rolled = pltpu.roll(base, 0, 1, stride=1, stride_axis=0)
                matrices[turn, n % 2, :, g * length : (g + 1) * length] = jnp.where(
                    keeps[turn], rolled, 0.0
                ).astype(BF16)
            matrix_copy(n, turn).start()
        return carry

    matrix_steps = groups // step
    lax.fori_loop(0, matrix_steps, matrix_step, 0)
    for n in range(max(matrix_steps - 2, 0), matrix_steps):
        for turn in range(2):
            matrix_copy(n, turn).wait()

    def sums_copy(n):
        slot = n % 2
        lanes = pl.ds(pl.multiple_of(n % blocks * width, width), width)
        return pltpu.make_async_copy(
            sums.at[slot], so_far_ref.at[n // blocks, :, lanes], sums_sem.at[slot]
        )

    def sums_step(n, carry):
        own_copy(n).wait()

        @pl.when(n >= 2)
        def _():
            sums_copy(n - 2).wait()

        lanes = pl.ds(pl.multiple_of(n % blocks * width, width), width)
        sums[n % 2] = jnp.dot(
            x_ref[...],
            held_ref[n // blocks, pl.ds(own_row, depth), lanes],
            preferred_element_type=F32,
        )
        sums_copy(n).start()
        return carry

    lax.fori_loop(0, 3 * blocks, sums_step, 0)
    for n in range(3 * blocks - 2, 3 * blocks):
        sums_copy(n).wait()
    for copy in rest:
        copy.wait()


def load(me, x, weights, medium, members):
    rows, depth = x.shape
    channels = weights.shape[2]
    length, groups = medium.shape
    width = min(512, channels)
    rest_rows = min(512, depth)
    matrix = jax.ShapeDtypeStruct((length, groups * length), BF16)
    return pl.pallas_call(
        functools.partial(load_kernel, members=members, width=width, rest_rows=rest_rows),
        in_specs=[IN_SMEM, IN_VMEM, ANYWHERE, IN_VMEM],
        out_specs=[IN_VMEM, ANYWHERE, ANYWHERE, ANYWHERE],
        out_shape=[
            pltpu.VMEM(weights.shape, BF16),
            jax.ShapeDtypeStruct((3, rows, channels), F32),
            matrix,
            matrix,
        ],
        scratch_shapes=[
            pltpu.VMEM((2, rows, width), F32),
            pltpu.VMEM((2, 2, length, 8 * length), BF16),
            pltpu.VMEM((2, groups, length), F32),
            pltpu.SemaphoreType.DMA((3 * channels // width,)),
            pltpu.SemaphoreType.DMA(((members - 1) * 3 * depth // rest_rows,)),
            pltpu.SemaphoreType.DMA((2,)),
            pltpu.SemaphoreType.DMA((2,)),
            pltpu.SemaphoreType.DMA((2,)),
        ],
        compiler_params=params(),
        cost_estimate=cost(6 * rows * depth * channels, 2 * weights.size),
        name="load",
    )(me, x, weights, medium)


STRIP = 8


def strip_filter(scratch, i, start, taps, micro, back):
    total = None
    for lag, tap in enumerate(taps):
        first = start + micro * (lag if back else -lag)
        term = tap * scratch[i, pl.ds(first, STRIP, stride=micro), :]
        total = term if total is None else total + term
    return total


def group_masks(members, width):
    group = lax.broadcasted_iota(jnp.int32, (1, width), 1) % LANES // members
    return [jnp.where(group == g, 1.0, 0.0).astype(BF16) for g in range(LANES // members)]


def mixer_kernel(
    me_ref, w_ref, taps_ref, skip_ref, grad_ref, so_far_ref, first_ref, second_ref, *rest,
    members, micro, group, width
):
    x_refs = rest[: members - 1]
    (
        out_ref, so_far, grads, first, second, lagged, keys, values, mixed_grads, rounded,
        so_far_sem, grads_sem, first_sem, second_sem,
    ) = rest[members - 1 :]
    rows, channels = out_ref.shape[1:]
    depth = x_refs[0].shape[1]
    me = me_ref[0]
    length = rows // micro
    reach = taps_ref.shape[0] * LANES // 3 // channels
    tiles = channels // LANES
    spread = LANES // group * length
    window = width // group * length
    blocks = channels // width
    pairs = length // (2 * STRIP)
    margin = micro * STRIP
    masks = group_masks(group, micro * LANES)

    def block_copies(n):
        slot = n % 2
        lanes = pl.ds(pl.multiple_of(n * width, width), width)
        return (
            pltpu.make_async_copy(
                so_far_ref.at[:, :, lanes], so_far.at[slot], so_far_sem.at[slot]
            ),
            pltpu.make_async_copy(grad_ref.at[:, lanes], grads.at[slot], grads_sem.at[slot]),
        )

    def matrix_copies(n):
        wide = pl.ds(pl.multiple_of(n * window, window), window)
        return (
            pltpu.make_async_copy(first_ref.at[:, wide], first, first_sem),
            pltpu.make_async_copy(second_ref.at[:, wide], second, second_sem),
        )

    def lanes_of(n, tile):
        return pl.ds(pl.multiple_of(n * width + tile * LANES, LANES), LANES)

    def project(n):
        lanes = pl.ds(pl.multiple_of(n * width, width), width)
        for i in range(3):
            total = so_far[n % 2, i]
            for k, x_ref in enumerate(x_refs):
                row = pl.multiple_of(lax.rem(me + k + 1, members) * depth, depth)
                total = total + jnp.dot(
                    x_ref[...], w_ref[i, pl.ds(row, depth), lanes], preferred_element_type=F32
                )
            for tile in range(width // LANES):
                for b in range(micro):
                    for start in range(0, length, STRIP):
                        first_row = margin + micro * start + b
                        lagged[tile, i, pl.ds(first_row, STRIP, stride=micro), :] = total[
                            b * length + start : b * length + start + STRIP,
                            tile * LANES : (tile + 1) * LANES,
                        ]

    def forward(n, tile, taps):
        inner = slice(tile * LANES, (tile + 1) * LANES)
        scratch = lagged.at[tile]
        for b in range(micro):
            place = slice(b * LANES, (b + 1) * LANES)
            for pair in range(pairs):
                start = pair * 2 * STRIP
                span = slice(b * length + start, b * length + start + 2 * STRIP)
                upstream = grads[n % 2, span, inner].astype(F32)
                products, backs = [], []
                for half in range(2):
                    time = start + half * STRIP
                    query, key, value = (
                        strip_filter(scratch, i, margin + micro * time + b, taps[i], micro, False)
                        for i in range(3)
                    )
                    mixed_grad = upstream[half * STRIP : (half + 1) * STRIP] * query
                    own = slice(b * length + time, b * length + time + STRIP)
                    keys[own, inner] = key
                    values[own, inner] = value
                    mixed_grads[own, inner] = mixed_grad
                    products.append(key * value)
                    backs.append(mixed_grad)
                held_rows = slice(start, start + 2 * STRIP)
                rounded[0, tile, held_rows, place] = jnp.concatenate(products, axis=0).astype(BF16)
                rounded[1, tile, held_rows, place] = jnp.concatenate(backs, axis=0).astype(BF16)

    def medium(tile):
        places = slice(tile * spread, (tile + 1) * spread)
        return [
            jnp.dot(
                matrix[:, places],
                jnp.concatenate([rounded[turn, tile] * mask for mask in masks], axis=0),
                preferred_element_type=F32,
            )
            for turn, matrix in enumerate((first, second))
        ]

    def backward(n, tile, taps, mixed, product_grad):
        inner = slice(tile * LANES, (tile + 1) * LANES)
        lanes = lanes_of(n, tile)
        scratch = lagged.at[tile]
        skip = jnp.broadcast_to(skip_ref[0:1, lanes], (STRIP, LANES))
        for b in range(micro):
            place = slice(b * LANES, (b + 1) * LANES)
            for pair in range(pairs):
                start = pair * 2 * STRIP
                span = slice(b * length + start, b * length + start + 2 * STRIP)
                upstream = grads[n % 2, span, inner].astype(F32)
                for half in range(2):
                    time = start + half * STRIP
                    own = slice(b * length + time, b * length + time + STRIP)
                    here = slice(time, time + STRIP)
                    key, value = keys[own, inner], values[own, inner]
                    back = product_grad[here, place] + skip * mixed_grads[own, inner]
                    streams = (
                        upstream[half * STRIP : (half + 1) * STRIP]
                        * (mixed[here, place] + skip * (key * value)),
                        back * value,
                        back * key,
                    )
                    for i in range(3):
                        first_row = margin + micro * time + b
                        scratch[i, pl.ds(first_row, STRIP, stride=micro), :] = streams[i]
        for b in range(micro):
            for start in range(0, length, 2 * STRIP):
                span = slice(b * length + start, b * length + start + 2 * STRIP)
                for i in range(3):
                    strips = [
                        strip_filter(
                            scratch, i, margin + micro * (start + half) + b, taps[i], micro, True
                        )
                        for half in (0, STRIP)
                    ]
                    out_ref[i, span, lanes] = jnp.concatenate(strips, axis=0).astype(BF16)

    for copy in block_copies(0):
        copy.start()
    zeros = jnp.zeros((width // LANES, 3, margin, LANES), F32)
    lagged[:, :, :margin, :] = zeros
    lagged[:, :, margin + micro * length :, :] = zeros

    def step(n, carry):
        @pl.when(n + 1 < blocks)
        def _():
            for copy in block_copies(n + 1):
                copy.start()

        for copy in matrix_copies(n):
            copy.start()
        for copy in block_copies(n):
            copy.wait()
        taps = []
        for tile in range(width // LANES):
            line = n * (width // LANES) + tile
            taps.append([
                [
                    jnp.broadcast_to(
                        taps_ref[pl.ds((j * 3 + i) * tiles + line, 1), :], (STRIP, LANES)
                    )
                    for j in range(reach)
                ]
                for i in range(3)
            ])
        project(n)
        for tile in range(width // LANES):
            forward(n, tile, taps[tile])
        for copy in matrix_copies(n):
            copy.wait()
        for tile in range(width // LANES):
            backward(n, tile, taps[tile], *medium(tile))
        return carry

    lax.fori_loop(0, blocks, step, 0)


def mixer(me, weights, taps, skip, grad, so_far, first, second, others, micro):
    rows, channels = so_far.shape[1:]
    members = len(others) + 1
    length = rows // micro
    groups = first.shape[1] // length
    group = channels // groups
    width = min(256, channels)
    window = width // group * length
    tiles = width // LANES
    return pl.pallas_call(
        functools.partial(
            mixer_kernel, members=members, micro=micro, group=group, width=width
        ),
        in_specs=[IN_SMEM] + [IN_VMEM] * 3 + [ANYWHERE] * 4 + [IN_VMEM] * len(others),
        out_specs=IN_VMEM,
        out_shape=pltpu.VMEM(so_far.shape, BF16),
        scratch_shapes=[
            pltpu.VMEM((2, 3, rows, width), F32),
            pltpu.VMEM((2, rows, width), BF16),
            pltpu.VMEM((length, window), BF16),
            pltpu.VMEM((length, window), BF16),
            pltpu.VMEM((tiles, 3, micro * (length + 2 * STRIP), LANES), F32),
            pltpu.VMEM((rows, width), F32),
            pltpu.VMEM((rows, width), F32),
            pltpu.VMEM((rows, width), F32),
            pltpu.VMEM((2, tiles, length, micro * LANES), BF16),
            pltpu.SemaphoreType.DMA((2,)),
            pltpu.SemaphoreType.DMA((2,)),
            pltpu.SemaphoreType.DMA,
            pltpu.SemaphoreType.DMA,
        ],
        compiler_params=params(),
        cost_estimate=cost(0, 18 * rows * channels),
        name="mixer",
    )(me, held(weights), taps, skip, grad, so_far, first, second, *map(held, others))


def input_grad_kernel(member_ref, conv_ref, w_ref, *rest, first, depth, width, with_grad):
    out_ref = rest[-1]
    start = member_ref[0] * depth + first
    for step in range(out_ref.shape[1] // width):
        place = slice(step * width, (step + 1) * width)
        row = pl.multiple_of(start + step * width, width)
        total = None
        for i in range(3):
            term = lax.dot_general(
                w_ref[i, pl.ds(row, width), :],
                conv_ref[i],
                (((1,), (1,)), ((), ())),
                preferred_element_type=F32,
            )
            total = term if total is None else total + term
        total = total.T
        if with_grad:
            total = total + rest[0][:, first + step * width : first + (step + 1) * width].astype(F32)
        out_ref[:, place] = total.astype(BF16)


def input_grad(conv, weights, member, first, extent, depth, grad=None, after=()):
    rows = conv.shape[1]
    operands = [conv, weights] + ([] if grad is None else [grad])
    return pl.pallas_call(
        functools.partial(
            input_grad_kernel, first=first, depth=depth, width=SPAN, with_grad=grad is not None
        ),
        in_specs=[IN_SMEM] + [IN_VMEM] * (len(operands) + len(after)),
        out_specs=IN_VMEM,
        out_shape=jax.ShapeDtypeStruct((rows, extent), BF16),
        compiler_params=params(),
        cost_estimate=cost(1, 1),
        name="input_grad",
    )(member, held(conv), held(weights), *operands[2:], *map(held, after))


def join(pieces, depth):
    rows = pieces[0][1].shape[0]

    def kernel(*refs):
        out_ref = refs[-1]
        for start in range(0, depth, SPAN):
            total = None
            for (first, piece), ref in zip(pieces, refs):
                if first <= start < first + piece.shape[1]:
                    term = ref[:, start - first : start - first + SPAN].astype(F32)
                    total = term if total is None else total + term
            out_ref[:, start : start + SPAN] = total.astype(BF16)

    return pl.pallas_call(
        kernel,
        out_shape=jax.ShapeDtypeStruct((rows, depth), BF16),
        compiler_params=params(),
        cost_estimate=cost(0, 6 * rows * depth),
        name="join",
    )(*[piece for _, piece in pieces])


def cuts_of(eighths, depth):
    step = depth // 8
    if step % SPAN:
        return [(0, depth)]
    first, spans = 0, []
    for count in eighths:
        spans.append((first, count * step))
        first += count * step
    return spans


def local(block_input, incoming, in_weight, short_taps, medium_taps, skip_weight):
    micro, length, depth = block_input.shape[1:]
    rows = micro * length
    members = lax.axis_size("tp")
    sections = lax.axis_size("section")
    me = lax.axis_index("tp")
    weights = jnp.transpose(in_weight[0], (1, 0, 2))
    x = block_input.reshape(rows, depth)
    grad = incoming.reshape(rows, depth)

    def owner(step):
        return jnp.full((1,), lax.rem(me + step, members), jnp.int32)

    others = []
    for k in range(1, members):
        pairs = [((m + k) % members, m) for m in range(members)]
        others.append(lax.ppermute(x, "tp", pairs))
    weights, so_far, first, second = load(owner(0), x, weights, medium_taps[0], members)
    conv = mixer(
        owner(0), weights, short_taps.reshape(-1, LANES), skip_weight, grad, so_far, first,
        second, others, micro,
    )
    pieces = []
    for k in list(range(1, members)) + [0]:
        pairs = [
            (s * members + m, (s - 1) % sections * members + (m + k) % members)
            for s in range(sections)
            for m in range(members)
        ]
        cuts = cuts_of(AWAY_CUTS if k else OWN_CUTS, depth)
        for first_column, extent in cuts:
            last = k == 0 and first_column + extent == depth and members > 1
            share = input_grad(
                conv, weights, owner(k), first_column, extent, depth,
                None if k else grad, (pieces[0][1],) if last else (),
            )
            pieces.append((first_column, lax.ppermute(share, ("section", "tp"), pairs)))
    return join(pieces, depth).reshape(block_input.shape)


def solution(mesh):
    in_specs = (
        P("section", None, None, "tp"),
        P("section", None, None, "tp"),
        P("section", None, None, "tp"),
        P("section", None, None, "tp"),
        P("section", None, "tp"),
        P("section", "tp"),
    )
    out_specs = P("section", None, None, "tp")
    return jax.shard_map(local, mesh=mesh, in_specs=in_specs, out_specs=out_specs, check_vma=False)
```

```python
import functools

import jax
import jax.numpy as jnp
from jax import lax
from jax.experimental import pallas as pl
from jax.experimental.pallas import tpu as pltpu
from jax.sharding import PartitionSpec as P

F32 = jnp.float32
BF16 = jnp.bfloat16
LANES = 128
MIB = 1024 * 1024
VMEM_LIMIT = 8 * MIB
SPAN = 256
AWAY_CUTS = (3, 5)
OWN_CUTS = (5, 3)

IN_VMEM = pl.BlockSpec(memory_space=pltpu.VMEM)
IN_SMEM = pl.BlockSpec(memory_space=pltpu.SMEM)
ANYWHERE = pl.BlockSpec(memory_space=pl.ANY)


def params():
    return pltpu.CompilerParams(vmem_limit_bytes=VMEM_LIMIT)


def cost(flops, moved):
    return pl.CostEstimate(flops=flops, bytes_accessed=moved, transcendentals=0)


def held(array):
    return pltpu.with_memory_space_constraint(array, pltpu.VMEM)


def load_kernel(
    me_ref, x_ref, w_ref, medium_ref, held_ref, so_far_ref, first_ref, second_ref,
    sums, matrices, turned_ref, own_sem, rest_sem, sums_sem, first_sem, second_sem,
    *, members, width, rest_rows
):
    rows, depth = x_ref.shape
    channels = w_ref.shape[2]
    length, groups = medium_ref.shape
    me = me_ref[0]
    own_row = pl.multiple_of(me * depth, depth)
    blocks = channels // width

    def own_copy(n):
        place = (
            n // blocks,
            pl.ds(own_row, depth),
            pl.ds(pl.multiple_of(n % blocks * width, width), width),
        )
        return pltpu.make_async_copy(w_ref.at[place], held_ref.at[place], own_sem.at[n])

    rest = []
    for k in range(1, members):
        row = pl.multiple_of(lax.rem(me + k, members) * depth, depth)
        for i in range(3):
            for part in range(depth // rest_rows):
                place = (i, pl.ds(pl.multiple_of(row + part * rest_rows, rest_rows), rest_rows))
                rest.append(
                    pltpu.make_async_copy(
                        w_ref.at[place], held_ref.at[place], rest_sem.at[len(rest)]
                    )
                )
    for n in range(3 * blocks):
        own_copy(n).start()
    for copy in rest:
        copy.start()

    places = lax.broadcasted_iota(jnp.int32, (length, length), 0)
    lags = lax.broadcasted_iota(jnp.int32, (length, length), 1)
    medium = medium_ref[...].astype(BF16)
    turns = (places == lags, (places + lags) % length == 0)
    for n, turn in enumerate(turns):
        turned_ref[n] = lax.dot_general(
            medium,
            jnp.where(turn, 1.0, 0.0).astype(BF16),
            (((0,), (0,)), ((), ())),
            preferred_element_type=F32,
        )
    step = 8
    keeps = (lags >= places, lags <= places)
    targets = (second_ref, first_ref)
    target_sems = (second_sem, first_sem)

    def matrix_copy(n, turn):
        slot = n % 2
        lanes = pl.ds(pl.multiple_of(n * step * length, step * length), step * length)
        return pltpu.make_async_copy(
            matrices.at[turn, slot], targets[turn].at[:, lanes], target_sems[turn].at[slot]
        )

    def matrix_step(n, carry):
        for turn in range(2):
            @pl.when(n >= 2)
            def _():
                matrix_copy(n - 2, turn).wait()

            lines = turned_ref[turn, pl.ds(pl.multiple_of(n * step, step), step), :]
            for g in range(step):
                base = jnp.broadcast_to(lines[g : g + 1], (length, length))
                rolled = pltpu.roll(base, 0, 1, stride=1, stride_axis=0)
                matrices[turn, n % 2, :, g * length : (g + 1) * length] = jnp.where(
                    keeps[turn], rolled, 0.0
                ).astype(BF16)
            matrix_copy(n, turn).start()
        return carry

    matrix_steps = groups // step
    lax.fori_loop(0, matrix_steps, matrix_step, 0)
    for n in range(max(matrix_steps - 2, 0), matrix_steps):
        for turn in range(2):
            matrix_copy(n, turn).wait()

    def sums_copy(n):
        slot = n % 2
        lanes = pl.ds(pl.multiple_of(n % blocks * width, width), width)
        return pltpu.make_async_copy(
            sums.at[slot], so_far_ref.at[n // blocks, :, lanes], sums_sem.at[slot]
        )

    def sums_step(n, carry):
        own_copy(n).wait()

        @pl.when(n >= 2)
        def _():
            sums_copy(n - 2).wait()

        lanes = pl.ds(pl.multiple_of(n % blocks * width, width), width)
        sums[n % 2] = jnp.dot(
            x_ref[...],
            held_ref[n // blocks, pl.ds(own_row, depth), lanes],
            preferred_element_type=F32,
        )
        sums_copy(n).start()
        return carry

    lax.fori_loop(0, 3 * blocks, sums_step, 0)
    for n in range(3 * blocks - 2, 3 * blocks):
        sums_copy(n).wait()
    for copy in rest:
        copy.wait()


def load(me, x, weights, medium, members):
    rows, depth = x.shape
    channels = weights.shape[2]
    length, groups = medium.shape
    width = min(512, channels)
    rest_rows = min(512, depth)
    matrix = jax.ShapeDtypeStruct((length, groups * length), BF16)
    return pl.pallas_call(
        functools.partial(load_kernel, members=members, width=width, rest_rows=rest_rows),
        in_specs=[IN_SMEM, IN_VMEM, ANYWHERE, IN_VMEM],
        out_specs=[IN_VMEM, ANYWHERE, ANYWHERE, ANYWHERE],
        out_shape=[
            pltpu.VMEM(weights.shape, BF16),
            jax.ShapeDtypeStruct((3, rows, channels), F32),
            matrix,
            matrix,
        ],
        scratch_shapes=[
            pltpu.VMEM((2, rows, width), F32),
            pltpu.VMEM((2, 2, length, 8 * length), BF16),
            pltpu.VMEM((2, groups, length), F32),
            pltpu.SemaphoreType.DMA((3 * channels // width,)),
            pltpu.SemaphoreType.DMA(((members - 1) * 3 * depth // rest_rows,)),
            pltpu.SemaphoreType.DMA((2,)),
            pltpu.SemaphoreType.DMA((2,)),
            pltpu.SemaphoreType.DMA((2,)),
        ],
        compiler_params=params(),
        cost_estimate=cost(6 * rows * depth * channels, 2 * weights.size),
        name="load",
    )(me, x, weights, medium)


STRIP = 8


def strip_filter(scratch, i, start, taps, micro, back):
    total = None
    for lag, tap in enumerate(taps):
        first = start + micro * (lag if back else -lag)
        term = tap * scratch[i, pl.ds(first, STRIP, stride=micro), :]
        total = term if total is None else total + term
    return total


def group_masks(members, width):
    group = lax.broadcasted_iota(jnp.int32, (1, width), 1) % LANES // members
    return [jnp.where(group == g, 1.0, 0.0).astype(BF16) for g in range(LANES // members)]


def mixer_kernel(
    me_ref, w_ref, taps_ref, skip_ref, grad_ref, so_far_ref, first_ref, second_ref, *rest,
    members, micro, group, width
):
    x_refs = rest[: members - 1]
    (
        out_ref, so_far, grads, first, second, lagged, keys, values, mixed_grads, rounded,
        so_far_sem, grads_sem, first_sem, second_sem,
    ) = rest[members - 1 :]
    rows, channels = out_ref.shape[1:]
    depth = x_refs[0].shape[1]
    me = me_ref[0]
    length = rows // micro
    reach = taps_ref.shape[0] * LANES // 3 // channels
    tiles = channels // LANES
    spread = LANES // group * length
    window = width // group * length
    blocks = channels // width
    pairs = length // (2 * STRIP)
    margin = micro * STRIP
    masks = group_masks(group, micro * LANES)

    def block_copies(n):
        slot = n % 2
        lanes = pl.ds(pl.multiple_of(n * width, width), width)
        return (
            pltpu.make_async_copy(
                so_far_ref.at[:, :, lanes], so_far.at[slot], so_far_sem.at[slot]
            ),
            pltpu.make_async_copy(grad_ref.at[:, lanes], grads.at[slot], grads_sem.at[slot]),
        )

    def matrix_copies(n):
        wide = pl.ds(pl.multiple_of(n * window, window), window)
        return (
            pltpu.make_async_copy(first_ref.at[:, wide], first, first_sem),
            pltpu.make_async_copy(second_ref.at[:, wide], second, second_sem),
        )

    def lanes_of(n, tile):
        return pl.ds(pl.multiple_of(n * width + tile * LANES, LANES), LANES)

    def project(n):
        lanes = pl.ds(pl.multiple_of(n * width, width), width)
        for i in range(3):
            total = so_far[n % 2, i]
            for k, x_ref in enumerate(x_refs):
                row = pl.multiple_of(lax.rem(me + k + 1, members) * depth, depth)
                total = total + jnp.dot(
                    x_ref[...], w_ref[i, pl.ds(row, depth), lanes], preferred_element_type=F32
                )
            for tile in range(width // LANES):
                for b in range(micro):
                    for start in range(0, length, STRIP):
                        first_row = margin + micro * start + b
                        lagged[tile, i, pl.ds(first_row, STRIP, stride=micro), :] = total[
                            b * length + start : b * length + start + STRIP,
                            tile * LANES : (tile + 1) * LANES,
                        ]

    def forward(n, tile, taps):
        inner = slice(tile * LANES, (tile + 1) * LANES)
        scratch = lagged.at[tile]
        for b in range(micro):
            place = slice(b * LANES, (b + 1) * LANES)
            for pair in range(pairs):
                start = pair * 2 * STRIP
                span = slice(b * length + start, b * length + start + 2 * STRIP)
                upstream = grads[n % 2, span, inner].astype(F32)
                products, backs = [], []
                for half in range(2):
                    time = start + half * STRIP
                    query, key, value = (
                        strip_filter(scratch, i, margin + micro * time + b, taps[i], micro, False)
                        for i in range(3)
                    )
                    mixed_grad = upstream[half * STRIP : (half + 1) * STRIP] * query
                    own = slice(b * length + time, b * length + time + STRIP)
                    keys[own, inner] = key
                    values[own, inner] = value
                    mixed_grads[own, inner] = mixed_grad
                    products.append(key * value)
                    backs.append(mixed_grad)
                held_rows = slice(start, start + 2 * STRIP)
                rounded[0, tile, held_rows, place] = jnp.concatenate(products, axis=0).astype(BF16)
                rounded[1, tile, held_rows, place] = jnp.concatenate(backs, axis=0).astype(BF16)

    def medium(tile):
        places = slice(tile * spread, (tile + 1) * spread)
        return [
            jnp.dot(
                matrix[:, places],
                jnp.concatenate([rounded[turn, tile] * mask for mask in masks], axis=0),
                preferred_element_type=F32,
            )
            for turn, matrix in enumerate((first, second))
        ]

    def backward(n, tile, taps, mixed, product_grad):
        inner = slice(tile * LANES, (tile + 1) * LANES)
        lanes = lanes_of(n, tile)
        scratch = lagged.at[tile]
        skip = jnp.broadcast_to(skip_ref[0:1, lanes], (STRIP, LANES))
        for b in range(micro):
            place = slice(b * LANES, (b + 1) * LANES)
            for pair in range(pairs):
                start = pair * 2 * STRIP
                span = slice(b * length + start, b * length + start + 2 * STRIP)
                upstream = grads[n % 2, span, inner].astype(F32)
                for half in range(2):
                    time = start + half * STRIP
                    own = slice(b * length + time, b * length + time + STRIP)
                    here = slice(time, time + STRIP)
                    key, value = keys[own, inner], values[own, inner]
                    back = product_grad[here, place] + skip * mixed_grads[own, inner]
                    streams = (
                        upstream[half * STRIP : (half + 1) * STRIP]
                        * (mixed[here, place] + skip * (key * value)),
                        back * value,
                        back * key,
                    )
                    for i in range(3):
                        first_row = margin + micro * time + b
                        scratch[i, pl.ds(first_row, STRIP, stride=micro), :] = streams[i]
        for b in range(micro):
            for start in range(0, length, 2 * STRIP):
                span = slice(b * length + start, b * length + start + 2 * STRIP)
                for i in range(3):
                    strips = [
                        strip_filter(
                            scratch, i, margin + micro * (start + half) + b, taps[i], micro, True
                        )
                        for half in (0, STRIP)
                    ]
                    out_ref[i, span, lanes] = jnp.concatenate(strips, axis=0).astype(BF16)

    for copy in block_copies(0):
        copy.start()
    zeros = jnp.zeros((width // LANES, 3, margin, LANES), F32)
    lagged[:, :, :margin, :] = zeros
    lagged[:, :, margin + micro * length :, :] = zeros

    def step(n, carry):
        @pl.when(n + 1 < blocks)
        def _():
            for copy in block_copies(n + 1):
                copy.start()

        for copy in matrix_copies(n):
            copy.start()
        for copy in block_copies(n):
            copy.wait()
        taps = []
        for tile in range(width // LANES):
            line = n * (width // LANES) + tile
            taps.append([
                [
                    jnp.broadcast_to(
                        taps_ref[pl.ds((j * 3 + i) * tiles + line, 1), :], (STRIP, LANES)
                    )
                    for j in range(reach)
                ]
                for i in range(3)
            ])
        project(n)
        for tile in range(width // LANES):
            forward(n, tile, taps[tile])
        for copy in matrix_copies(n):
            copy.wait()
        for tile in range(width // LANES):
            backward(n, tile, taps[tile], *medium(tile))
        return carry

    lax.fori_loop(0, blocks, step, 0)


def mixer(me, weights, taps, skip, grad, so_far, first, second, others, micro):
    rows, channels = so_far.shape[1:]
    members = len(others) + 1
    length = rows // micro
    groups = first.shape[1] // length
    group = channels // groups
    width = min(256, channels)
    window = width // group * length
    tiles = width // LANES
    return pl.pallas_call(
        functools.partial(
            mixer_kernel, members=members, micro=micro, group=group, width=width
        ),
        in_specs=[IN_SMEM] + [IN_VMEM] * 3 + [ANYWHERE] * 4 + [IN_VMEM] * len(others),
        out_specs=IN_VMEM,
        out_shape=pltpu.VMEM(so_far.shape, BF16),
        scratch_shapes=[
            pltpu.VMEM((2, 3, rows, width), F32),
            pltpu.VMEM((2, rows, width), BF16),
            pltpu.VMEM((length, window), BF16),
            pltpu.VMEM((length, window), BF16),
            pltpu.VMEM((tiles, 3, micro * (length + 2 * STRIP), LANES), F32),
            pltpu.VMEM((rows, width), F32),
            pltpu.VMEM((rows, width), F32),
            pltpu.VMEM((rows, width), F32),
            pltpu.VMEM((2, tiles, length, micro * LANES), BF16),
            pltpu.SemaphoreType.DMA((2,)),
            pltpu.SemaphoreType.DMA((2,)),
            pltpu.SemaphoreType.DMA,
            pltpu.SemaphoreType.DMA,
        ],
        compiler_params=params(),
        cost_estimate=cost(0, 18 * rows * channels),
        name="mixer",
    )(me, held(weights), taps, skip, grad, so_far, first, second, *map(held, others))


def input_grad_kernel(member_ref, conv_ref, w_ref, *rest, first, depth, width, with_grad):
    out_ref = rest[-1]
    start = member_ref[0] * depth + first
    for step in range(out_ref.shape[1] // width):
        place = slice(step * width, (step + 1) * width)
        row = pl.multiple_of(start + step * width, width)
        total = None
        for i in range(3):
            term = lax.dot_general(
                w_ref[i, pl.ds(row, width), :],
                conv_ref[i],
                (((1,), (1,)), ((), ())),
                preferred_element_type=F32,
            )
            total = term if total is None else total + term
        total = total.T
        if with_grad:
            total = total + rest[0][:, first + step * width : first + (step + 1) * width].astype(F32)
        out_ref[:, place] = total.astype(BF16)


def input_grad(conv, weights, member, first, extent, depth, grad=None, after=()):
    rows = conv.shape[1]
    operands = [conv, weights] + ([] if grad is None else [grad])
    return pl.pallas_call(
        functools.partial(
            input_grad_kernel, first=first, depth=depth, width=SPAN, with_grad=grad is not None
        ),
        in_specs=[IN_SMEM] + [IN_VMEM] * (len(operands) + len(after)),
        out_specs=IN_VMEM,
        out_shape=jax.ShapeDtypeStruct((rows, extent), BF16),
        compiler_params=params(),
        cost_estimate=cost(1, 1),
        name="input_grad",
    )(member, held(conv), held(weights), *map(held, operands[2:]), *map(held, after))


def join(pieces, depth):
    rows = pieces[0][1].shape[0]

    def kernel(*refs):
        out_ref = refs[-1]
        for start in range(0, depth, SPAN):
            total = None
            for (first, piece), ref in zip(pieces, refs):
                if first <= start < first + piece.shape[1]:
                    term = ref[:, start - first : start - first + SPAN].astype(F32)
                    total = term if total is None else total + term
            out_ref[:, start : start + SPAN] = total.astype(BF16)

    return pl.pallas_call(
        kernel,
        out_shape=jax.ShapeDtypeStruct((rows, depth), BF16),
        compiler_params=params(),
        cost_estimate=cost(0, 6 * rows * depth),
        name="join",
    )(*[piece for _, piece in pieces])


def cuts_of(eighths, depth):
    step = depth // 8
    if step % SPAN:
        return [(0, depth)]
    first, spans = 0, []
    for count in eighths:
        spans.append((first, count * step))
        first += count * step
    return spans


def local(block_input, incoming, in_weight, short_taps, medium_taps, skip_weight):
    micro, length, depth = block_input.shape[1:]
    rows = micro * length
    members = lax.axis_size("tp")
    sections = lax.axis_size("section")
    me = lax.axis_index("tp")
    weights = jnp.transpose(in_weight[0], (1, 0, 2))
    x = block_input.reshape(rows, depth)
    grad = incoming.reshape(rows, depth)

    def owner(step):
        return jnp.full((1,), lax.rem(me + step, members), jnp.int32)

    others = []
    for k in range(1, members):
        pairs = [((m + k) % members, m) for m in range(members)]
        others.append(lax.ppermute(x, "tp", pairs))
    weights, so_far, first, second = load(owner(0), x, weights, medium_taps[0], members)
    conv = mixer(
        owner(0), weights, short_taps.reshape(-1, LANES), skip_weight, grad, so_far, first,
        second, others, micro,
    )
    pieces = []
    for k in list(range(1, members)) + [0]:
        pairs = [
            (s * members + m, (s - 1) % sections * members + (m + k) % members)
            for s in range(sections)
            for m in range(members)
        ]
        cuts = cuts_of(AWAY_CUTS if k else OWN_CUTS, depth)
        for first_column, extent in cuts:
            last = k == 0 and first_column + extent == depth and members > 1
            share = input_grad(
                conv, weights, owner(k), first_column, extent, depth,
                None if k else grad, (pieces[0][1],) if last else (),
            )
            pieces.append((first_column, lax.ppermute(share, ("section", "tp"), pairs)))
    return join(pieces, depth).reshape(block_input.shape)


def solution(mesh):
    in_specs = (
        P("section", None, None, "tp"),
        P("section", None, None, "tp"),
        P("section", None, None, "tp"),
        P("section", None, None, "tp"),
        P("section", None, "tp"),
        P("section", "tp"),
    )
    out_specs = P("section", None, None, "tp")
    return jax.shard_map(local, mesh=mesh, in_specs=in_specs, out_specs=out_specs, check_vma=False)
```

```python
import functools

import jax
import jax.numpy as jnp
from jax import lax
from jax.experimental import pallas as pl
from jax.experimental.pallas import tpu as pltpu
from jax.sharding import PartitionSpec as P

F32 = jnp.float32
BF16 = jnp.bfloat16
LANES = 128
MIB = 1024 * 1024
VMEM_LIMIT = 8 * MIB
SPAN = 256
AWAY_CUTS = (3, 5)
OWN_CUTS = (5, 3)

IN_VMEM = pl.BlockSpec(memory_space=pltpu.VMEM)
IN_SMEM = pl.BlockSpec(memory_space=pltpu.SMEM)
ANYWHERE = pl.BlockSpec(memory_space=pl.ANY)


def params():
    return pltpu.CompilerParams(vmem_limit_bytes=VMEM_LIMIT)


def cost(flops, moved):
    return pl.CostEstimate(flops=flops, bytes_accessed=moved, transcendentals=0)


def held(array):
    return pltpu.with_memory_space_constraint(array, pltpu.VMEM)


def load_kernel(
    me_ref, x_ref, w_ref, medium_ref, held_ref, so_far_ref, first_ref, second_ref,
    sums, matrices, turned_ref, own_sem, rest_sem, sums_sem, first_sem, second_sem,
    *, members, width, rest_rows
):
    rows, depth = x_ref.shape
    channels = w_ref.shape[2]
    length, groups = medium_ref.shape
    me = me_ref[0]
    own_row = pl.multiple_of(me * depth, depth)
    blocks = channels // width

    def own_copy(n):
        place = (
            n // blocks,
            pl.ds(own_row, depth),
            pl.ds(pl.multiple_of(n % blocks * width, width), width),
        )
        return pltpu.make_async_copy(w_ref.at[place], held_ref.at[place], own_sem.at[n])

    rest = []
    for k in range(1, members):
        row = pl.multiple_of(lax.rem(me + k, members) * depth, depth)
        for i in range(3):
            for part in range(depth // rest_rows):
                place = (i, pl.ds(pl.multiple_of(row + part * rest_rows, rest_rows), rest_rows))
                rest.append(
                    pltpu.make_async_copy(
                        w_ref.at[place], held_ref.at[place], rest_sem.at[len(rest)]
                    )
                )
    for n in range(3 * blocks):
        own_copy(n).start()
    for copy in rest:
        copy.start()

    places = lax.broadcasted_iota(jnp.int32, (length, length), 0)
    lags = lax.broadcasted_iota(jnp.int32, (length, length), 1)
    medium = medium_ref[...].astype(BF16)
    turns = (places == lags, (places + lags) % length == 0)
    for n, turn in enumerate(turns):
        turned_ref[n] = lax.dot_general(
            medium,
            jnp.where(turn, 1.0, 0.0).astype(BF16),
            (((0,), (0,)), ((), ())),
            preferred_element_type=F32,
        )
    step = 8
    keeps = (lags >= places, lags <= places)
    targets = (second_ref, first_ref)
    target_sems = (second_sem, first_sem)

    def matrix_copy(n, turn):
        slot = n % 2
        lanes = pl.ds(pl.multiple_of(n * step * length, step * length), step * length)
        return pltpu.make_async_copy(
            matrices.at[turn, slot], targets[turn].at[:, lanes], target_sems[turn].at[slot]
        )

    def matrix_step(n, carry):
        for turn in range(2):
            @pl.when(n >= 2)
            def _():
                matrix_copy(n - 2, turn).wait()

            lines = turned_ref[turn, pl.ds(pl.multiple_of(n * step, step), step), :]
            for g in range(step):
                base = jnp.broadcast_to(lines[g : g + 1], (length, length))
                rolled = pltpu.roll(base, 0, 1, stride=1, stride_axis=0)
                matrices[turn, n % 2, :, g * length : (g + 1) * length] = jnp.where(
                    keeps[turn], rolled, 0.0
                ).astype(BF16)
            matrix_copy(n, turn).start()
        return carry

    matrix_steps = groups // step
    lax.fori_loop(0, matrix_steps, matrix_step, 0)
    for n in range(max(matrix_steps - 2, 0), matrix_steps):
        for turn in range(2):
            matrix_copy(n, turn).wait()

    def sums_copy(n):
        slot = n % 2
        lanes = pl.ds(pl.multiple_of(n % blocks * width, width), width)
        return pltpu.make_async_copy(
            sums.at[slot], so_far_ref.at[n // blocks, :, lanes], sums_sem.at[slot]
        )

    def sums_step(n, carry):
        own_copy(n).wait()

        @pl.when(n >= 2)
        def _():
            sums_copy(n - 2).wait()

        lanes = pl.ds(pl.multiple_of(n % blocks * width, width), width)
        sums[n % 2] = jnp.dot(
            x_ref[...],
            held_ref[n // blocks, pl.ds(own_row, depth), lanes],
            preferred_element_type=F32,
        )
        sums_copy(n).start()
        return carry

    lax.fori_loop(0, 3 * blocks, sums_step, 0)
    for n in range(3 * blocks - 2, 3 * blocks):
        sums_copy(n).wait()
    for copy in rest:
        copy.wait()


def load(me, x, weights, medium, members):
    rows, depth = x.shape
    channels = weights.shape[2]
    length, groups = medium.shape
    width = min(512, channels)
    rest_rows = min(512, depth)
    matrix = jax.ShapeDtypeStruct((length, groups * length), BF16)
    return pl.pallas_call(
        functools.partial(load_kernel, members=members, width=width, rest_rows=rest_rows),
        in_specs=[IN_SMEM, IN_VMEM, ANYWHERE, IN_VMEM],
        out_specs=[IN_VMEM, ANYWHERE, ANYWHERE, ANYWHERE],
        out_shape=[
            pltpu.VMEM(weights.shape, BF16),
            jax.ShapeDtypeStruct((3, rows, channels), F32),
            matrix,
            matrix,
        ],
        scratch_shapes=[
            pltpu.VMEM((2, rows, width), F32),
            pltpu.VMEM((2, 2, length, 8 * length), BF16),
            pltpu.VMEM((2, groups, length), F32),
            pltpu.SemaphoreType.DMA((3 * channels // width,)),
            pltpu.SemaphoreType.DMA(((members - 1) * 3 * depth // rest_rows,)),
            pltpu.SemaphoreType.DMA((2,)),
            pltpu.SemaphoreType.DMA((2,)),
            pltpu.SemaphoreType.DMA((2,)),
        ],
        compiler_params=params(),
        cost_estimate=cost(6 * rows * depth * channels, 2 * weights.size),
        name="load",
    )(me, x, weights, medium)


STRIP = 8


def strip_filter(scratch, i, start, taps, micro, back):
    total = None
    for lag, tap in enumerate(taps):
        first = start + micro * (lag if back else -lag)
        term = tap * scratch[i, pl.ds(first, STRIP, stride=micro), :]
        total = term if total is None else total + term
    return total


def group_masks(members, width):
    group = lax.broadcasted_iota(jnp.int32, (1, width), 1) % LANES // members
    return [jnp.where(group == g, 1.0, 0.0).astype(BF16) for g in range(LANES // members)]


def mixer_kernel(
    me_ref, w_ref, taps_ref, skip_ref, grad_ref, so_far_ref, first_ref, second_ref, *rest,
    members, micro, group, width, wide
):
    x_refs = rest[: members - 1]
    (
        out_ref, so_far, grads, first, second, lagged, keys, values, mixed_grads, rounded,
        so_far_sem, grads_sem, first_sem, second_sem,
    ) = rest[members - 1 :]
    rows, channels = out_ref.shape[1:]
    depth = x_refs[0].shape[1]
    me = me_ref[0]
    length = rows // micro
    reach = taps_ref.shape[0] * LANES // 3 // channels
    tiles = channels // LANES
    spread = LANES // group * length
    window = width // group * length
    blocks = channels // width
    ratio = wide // width
    pairs = length // (2 * STRIP)
    margin = micro * STRIP
    masks = group_masks(group, micro * LANES)

    def so_far_copy(m):
        lanes = pl.ds(pl.multiple_of(m * wide, wide), wide)
        return pltpu.make_async_copy(so_far_ref.at[:, :, lanes], so_far, so_far_sem)

    def grads_copy(n):
        slot = n % 2
        lanes = pl.ds(pl.multiple_of(n * width, width), width)
        return pltpu.make_async_copy(grad_ref.at[:, lanes], grads.at[slot], grads_sem.at[slot])

    def matrix_copies(n):
        places = pl.ds(pl.multiple_of(n * window, window), window)
        return (
            pltpu.make_async_copy(first_ref.at[:, places], first, first_sem),
            pltpu.make_async_copy(second_ref.at[:, places], second, second_sem),
        )

    def lanes_of(n, tile):
        return pl.ds(pl.multiple_of(n * width + tile * LANES, LANES), LANES)

    def project(m):
        lanes = pl.ds(pl.multiple_of(m * wide, wide), wide)
        for i in range(3):
            total = so_far[i]
            for k, x_ref in enumerate(x_refs):
                row = pl.multiple_of(lax.rem(me + k + 1, members) * depth, depth)
                total = total + jnp.dot(
                    x_ref[...], w_ref[i, pl.ds(row, depth), lanes], preferred_element_type=F32
                )
            for tile in range(wide // LANES):
                for b in range(micro):
                    for start in range(0, length, STRIP):
                        first_row = margin + micro * start + b
                        lagged[tile, i, pl.ds(first_row, STRIP, stride=micro), :] = total[
                            b * length + start : b * length + start + STRIP,
                            tile * LANES : (tile + 1) * LANES,
                        ]

    def forward(n, tile, taps):
        inner = slice(tile * LANES, (tile + 1) * LANES)
        scratch = lagged.at[n % ratio * (width // LANES) + tile]
        for b in range(micro):
            place = slice(b * LANES, (b + 1) * LANES)
            for pair in range(pairs):
                start = pair * 2 * STRIP
                span = slice(b * length + start, b * length + start + 2 * STRIP)
                upstream = grads[n % 2, span, inner].astype(F32)
                products, backs = [], []
                for half in range(2):
                    time = start + half * STRIP
                    query, key, value = (
                        strip_filter(scratch, i, margin + micro * time + b, taps[i], micro, False)
                        for i in range(3)
                    )
                    mixed_grad = upstream[half * STRIP : (half + 1) * STRIP] * query
                    own = slice(b * length + time, b * length + time + STRIP)
                    keys[own, inner] = key
                    values[own, inner] = value
                    mixed_grads[own, inner] = mixed_grad
                    products.append(key * value)
                    backs.append(mixed_grad)
                held_rows = slice(start, start + 2 * STRIP)
                rounded[0, tile, held_rows, place] = jnp.concatenate(products, axis=0).astype(BF16)
                rounded[1, tile, held_rows, place] = jnp.concatenate(backs, axis=0).astype(BF16)

    def medium(tile):
        places = slice(tile * spread, (tile + 1) * spread)
        return [
            jnp.dot(
                matrix[:, places],
                jnp.concatenate([rounded[turn, tile] * mask for mask in masks], axis=0),
                preferred_element_type=F32,
            )
            for turn, matrix in enumerate((first, second))
        ]

    def backward(n, tile, taps, mixed, product_grad):
        inner = slice(tile * LANES, (tile + 1) * LANES)
        lanes = lanes_of(n, tile)
        scratch = lagged.at[n % ratio * (width // LANES) + tile]
        skip = jnp.broadcast_to(skip_ref[0:1, lanes], (STRIP, LANES))
        for b in range(micro):
            place = slice(b * LANES, (b + 1) * LANES)
            for pair in range(pairs):
                start = pair * 2 * STRIP
                span = slice(b * length + start, b * length + start + 2 * STRIP)
                upstream = grads[n % 2, span, inner].astype(F32)
                for half in range(2):
                    time = start + half * STRIP
                    own = slice(b * length + time, b * length + time + STRIP)
                    here = slice(time, time + STRIP)
                    key, value = keys[own, inner], values[own, inner]
                    back = product_grad[here, place] + skip * mixed_grads[own, inner]
                    streams = (
                        upstream[half * STRIP : (half + 1) * STRIP]
                        * (mixed[here, place] + skip * (key * value)),
                        back * value,
                        back * key,
                    )
                    for i in range(3):
                        first_row = margin + micro * time + b
                        scratch[i, pl.ds(first_row, STRIP, stride=micro), :] = streams[i]
        for b in range(micro):
            for start in range(0, length, 2 * STRIP):
                span = slice(b * length + start, b * length + start + 2 * STRIP)
                for i in range(3):
                    strips = [
                        strip_filter(
                            scratch, i, margin + micro * (start + half) + b, taps[i], micro, True
                        )
                        for half in (0, STRIP)
                    ]
                    out_ref[i, span, lanes] = jnp.concatenate(strips, axis=0).astype(BF16)

    so_far_copy(0).start()
    grads_copy(0).start()
    zeros = jnp.zeros((wide // LANES, 3, margin, LANES), F32)
    lagged[:, :, :margin, :] = zeros
    lagged[:, :, margin + micro * length :, :] = zeros

    def step(n, carry):
        @pl.when(n + 1 < blocks)
        def _():
            grads_copy(n + 1).start()

        for copy in matrix_copies(n):
            copy.start()
        grads_copy(n).wait()
        taps = []
        for tile in range(width // LANES):
            line = n * (width // LANES) + tile
            taps.append([
                [
                    jnp.broadcast_to(
                        taps_ref[pl.ds((j * 3 + i) * tiles + line, 1), :], (STRIP, LANES)
                    )
                    for j in range(reach)
                ]
                for i in range(3)
            ])

        @pl.when(n % ratio == 0)
        def _():
            so_far_copy(n // ratio).wait()
            project(n // ratio)

            @pl.when(n + ratio < blocks)
            def _():
                so_far_copy(n // ratio + 1).start()

        for tile in range(width // LANES):
            forward(n, tile, taps[tile])
        for copy in matrix_copies(n):
            copy.wait()
        for tile in range(width // LANES):
            backward(n, tile, taps[tile], *medium(tile))
        return carry

    lax.fori_loop(0, blocks, step, 0)


def mixer(me, weights, taps, skip, grad, so_far, first, second, others, micro):
    rows, channels = so_far.shape[1:]
    members = len(others) + 1
    length = rows // micro
    groups = first.shape[1] // length
    group = channels // groups
    width = min(256, channels)
    window = width // group * length
    tiles = width // LANES
    wide = 2 * width if channels % (2 * width) == 0 else width
    return pl.pallas_call(
        functools.partial(
            mixer_kernel, members=members, micro=micro, group=group, width=width, wide=wide
        ),
        in_specs=[IN_SMEM] + [IN_VMEM] * 3 + [ANYWHERE] * 4 + [IN_VMEM] * len(others),
        out_specs=IN_VMEM,
        out_shape=pltpu.VMEM(so_far.shape, BF16),
        scratch_shapes=[
            pltpu.VMEM((3, rows, wide), F32),
            pltpu.VMEM((2, rows, width), BF16),
            pltpu.VMEM((length, window), BF16),
            pltpu.VMEM((length, window), BF16),
            pltpu.VMEM((wide // LANES, 3, micro * (length + 2 * STRIP), LANES), F32),
            pltpu.VMEM((rows, width), F32),
            pltpu.VMEM((rows, width), F32),
            pltpu.VMEM((rows, width), F32),
            pltpu.VMEM((2, tiles, length, micro * LANES), BF16),
            pltpu.SemaphoreType.DMA,
            pltpu.SemaphoreType.DMA((2,)),
            pltpu.SemaphoreType.DMA,
            pltpu.SemaphoreType.DMA,
        ],
        compiler_params=params(),
        cost_estimate=cost(0, 18 * rows * channels),
        name="mixer",
    )(me, held(weights), taps, skip, grad, so_far, first, second, *map(held, others))


def input_grad_kernel(member_ref, conv_ref, w_ref, *rest, first, depth, width, with_grad):
    out_ref = rest[-1]
    start = member_ref[0] * depth + first
    for step in range(out_ref.shape[1] // width):
        place = slice(step * width, (step + 1) * width)
        row = pl.multiple_of(start + step * width, width)
        total = None
        for i in range(3):
            term = lax.dot_general(
                w_ref[i, pl.ds(row, width), :],
                conv_ref[i],
                (((1,), (1,)), ((), ())),
                preferred_element_type=F32,
            )
            total = term if total is None else total + term
        total = total.T
        if with_grad:
            total = total + rest[0][:, first + step * width : first + (step + 1) * width].astype(F32)
        out_ref[:, place] = total.astype(BF16)


def input_grad(conv, weights, member, first, extent, depth, grad=None, after=()):
    rows = conv.shape[1]
    operands = [conv, weights] + ([] if grad is None else [grad])
    return pl.pallas_call(
        functools.partial(
            input_grad_kernel, first=first, depth=depth, width=SPAN, with_grad=grad is not None
        ),
        in_specs=[IN_SMEM] + [IN_VMEM] * (len(operands) + len(after)),
        out_specs=IN_VMEM,
        out_shape=jax.ShapeDtypeStruct((rows, extent), BF16),
        compiler_params=params(),
        cost_estimate=cost(1, 1),
        name="input_grad",
    )(member, held(conv), held(weights), *operands[2:], *map(held, after))


def join(pieces, depth):
    rows = pieces[0][1].shape[0]

    def kernel(*refs):
        out_ref = refs[-1]
        for start in range(0, depth, SPAN):
            total = None
            for (first, piece), ref in zip(pieces, refs):
                if first <= start < first + piece.shape[1]:
                    term = ref[:, start - first : start - first + SPAN].astype(F32)
                    total = term if total is None else total + term
            out_ref[:, start : start + SPAN] = total.astype(BF16)

    return pl.pallas_call(
        kernel,
        out_shape=jax.ShapeDtypeStruct((rows, depth), BF16),
        compiler_params=params(),
        cost_estimate=cost(0, 6 * rows * depth),
        name="join",
    )(*[piece for _, piece in pieces])


def cuts_of(eighths, depth):
    step = depth // 8
    if step % SPAN:
        return [(0, depth)]
    first, spans = 0, []
    for count in eighths:
        spans.append((first, count * step))
        first += count * step
    return spans


def local(block_input, incoming, in_weight, short_taps, medium_taps, skip_weight):
    micro, length, depth = block_input.shape[1:]
    rows = micro * length
    members = lax.axis_size("tp")
    sections = lax.axis_size("section")
    me = lax.axis_index("tp")
    weights = jnp.transpose(in_weight[0], (1, 0, 2))
    x = block_input.reshape(rows, depth)
    grad = incoming.reshape(rows, depth)

    def owner(step):
        return jnp.full((1,), lax.rem(me + step, members), jnp.int32)

    others = []
    for k in range(1, members):
        pairs = [((m + k) % members, m) for m in range(members)]
        others.append(lax.ppermute(x, "tp", pairs))
    weights, so_far, first, second = load(owner(0), x, weights, medium_taps[0], members)
    conv = mixer(
        owner(0), weights, short_taps.reshape(-1, LANES), skip_weight, grad, so_far, first,
        second, others, micro,
    )
    pieces = []
    for k in list(range(1, members)) + [0]:
        pairs = [
            (s * members + m, (s - 1) % sections * members + (m + k) % members)
            for s in range(sections)
            for m in range(members)
        ]
        cuts = cuts_of(AWAY_CUTS if k else OWN_CUTS, depth)
        for first_column, extent in cuts:
            last = k == 0 and first_column + extent == depth and members > 1
            share = input_grad(
                conv, weights, owner(k), first_column, extent, depth,
                None if k else grad, (pieces[0][1],) if last else (),
            )
            pieces.append((first_column, lax.ppermute(share, ("section", "tp"), pairs)))
    return join(pieces, depth).reshape(block_input.shape)


def solution(mesh):
    in_specs = (
        P("section", None, None, "tp"),
        P("section", None, None, "tp"),
        P("section", None, None, "tp"),
        P("section", None, None, "tp"),
        P("section", None, "tp"),
        P("section", "tp"),
    )
    out_specs = P("section", None, None, "tp")
    return jax.shard_map(local, mesh=mesh, in_specs=in_specs, out_specs=out_specs, check_vma=False)
```

```python
import functools

import jax
import jax.numpy as jnp
from jax import lax
from jax.experimental import pallas as pl
from jax.experimental.pallas import tpu as pltpu
from jax.sharding import PartitionSpec as P

F32 = jnp.float32
BF16 = jnp.bfloat16
LANES = 128
MIB = 1024 * 1024
VMEM_LIMIT = 8 * MIB
SPAN = 256
AWAY_CUTS = (3, 5)
OWN_CUTS = (5, 3)

IN_VMEM = pl.BlockSpec(memory_space=pltpu.VMEM)
IN_SMEM = pl.BlockSpec(memory_space=pltpu.SMEM)
ANYWHERE = pl.BlockSpec(memory_space=pl.ANY)


def params():
    return pltpu.CompilerParams(vmem_limit_bytes=VMEM_LIMIT)


def cost(flops, moved):
    return pl.CostEstimate(flops=flops, bytes_accessed=moved, transcendentals=0)


def held(array):
    return pltpu.with_memory_space_constraint(array, pltpu.VMEM)


def load_kernel(
    me_ref, x_ref, w_ref, medium_ref, held_ref, so_far_ref, first_ref, second_ref,
    sums, matrices, turned_ref, own_sem, rest_sem, sums_sem, first_sem, second_sem,
    *, members, width, rest_rows
):
    rows, depth = x_ref.shape
    channels = w_ref.shape[2]
    length, groups = medium_ref.shape
    me = me_ref[0]
    own_row = pl.multiple_of(me * depth, depth)
    blocks = channels // width

    def own_copy(n):
        place = (
            n // blocks,
            pl.ds(own_row, depth),
            pl.ds(pl.multiple_of(n % blocks * width, width), width),
        )
        return pltpu.make_async_copy(w_ref.at[place], held_ref.at[place], own_sem.at[n])

    rest = []
    for k in range(1, members):
        row = pl.multiple_of(lax.rem(me + k, members) * depth, depth)
        for i in range(3):
            for part in range(depth // rest_rows):
                place = (i, pl.ds(pl.multiple_of(row + part * rest_rows, rest_rows), rest_rows))
                rest.append(
                    pltpu.make_async_copy(
                        w_ref.at[place], held_ref.at[place], rest_sem.at[len(rest)]
                    )
                )
    for n in range(3 * blocks):
        own_copy(n).start()
    for copy in rest:
        copy.start()

    places = lax.broadcasted_iota(jnp.int32, (length, length), 0)
    lags = lax.broadcasted_iota(jnp.int32, (length, length), 1)
    medium = medium_ref[...].astype(BF16)
    turns = (places == lags, (places + lags) % length == 0)
    for n, turn in enumerate(turns):
        turned_ref[n] = lax.dot_general(
            medium,
            jnp.where(turn, 1.0, 0.0).astype(BF16),
            (((0,), (0,)), ((), ())),
            preferred_element_type=F32,
        )
    step = 8
    keeps = (lags >= places, lags <= places)
    targets = (second_ref, first_ref)
    target_sems = (second_sem, first_sem)

    def matrix_copy(n, turn):
        slot = n % 2
        lanes = pl.ds(pl.multiple_of(n * step * length, step * length), step * length)
        return pltpu.make_async_copy(
            matrices.at[turn, slot], targets[turn].at[:, lanes], target_sems[turn].at[slot]
        )

    def matrix_step(n, carry):
        for turn in range(2):
            @pl.when(n >= 2)
            def _():
                matrix_copy(n - 2, turn).wait()

            lines = turned_ref[turn, pl.ds(pl.multiple_of(n * step, step), step), :]
            for g in range(step):
                base = jnp.broadcast_to(lines[g : g + 1], (length, length))
                rolled = pltpu.roll(base, 0, 1, stride=1, stride_axis=0)
                matrices[turn, n % 2, :, g * length : (g + 1) * length] = jnp.where(
                    keeps[turn], rolled, 0.0
                ).astype(BF16)
            matrix_copy(n, turn).start()
        return carry

    matrix_steps = groups // step
    lax.fori_loop(0, matrix_steps, matrix_step, 0)
    for n in range(max(matrix_steps - 2, 0), matrix_steps):
        for turn in range(2):
            matrix_copy(n, turn).wait()

    def sums_copy(n):
        slot = n % 2
        lanes = pl.ds(pl.multiple_of(n % blocks * width, width), width)
        return pltpu.make_async_copy(
            sums.at[slot], so_far_ref.at[n // blocks, :, lanes], sums_sem.at[slot]
        )

    def sums_step(n, carry):
        own_copy(n).wait()

        @pl.when(n >= 2)
        def _():
            sums_copy(n - 2).wait()

        lanes = pl.ds(pl.multiple_of(n % blocks * width, width), width)
        sums[n % 2] = jnp.dot(
            x_ref[...],
            held_ref[n // blocks, pl.ds(own_row, depth), lanes],
            preferred_element_type=F32,
        )
        sums_copy(n).start()
        return carry

    lax.fori_loop(0, 3 * blocks, sums_step, 0)
    for n in range(3 * blocks - 2, 3 * blocks):
        sums_copy(n).wait()
    for copy in rest:
        copy.wait()


def load(me, x, weights, medium, members):
    rows, depth = x.shape
    channels = weights.shape[2]
    length, groups = medium.shape
    width = min(512, channels)
    rest_rows = min(512, depth)
    matrix = jax.ShapeDtypeStruct((length, groups * length), BF16)
    return pl.pallas_call(
        functools.partial(load_kernel, members=members, width=width, rest_rows=rest_rows),
        in_specs=[IN_SMEM, IN_VMEM, ANYWHERE, IN_VMEM],
        out_specs=[IN_VMEM, ANYWHERE, ANYWHERE, ANYWHERE],
        out_shape=[
            pltpu.VMEM(weights.shape, BF16),
            jax.ShapeDtypeStruct((3, rows, channels), F32),
            matrix,
            matrix,
        ],
        scratch_shapes=[
            pltpu.VMEM((2, rows, width), F32),
            pltpu.VMEM((2, 2, length, 8 * length), BF16),
            pltpu.VMEM((2, groups, length), F32),
            pltpu.SemaphoreType.DMA((3 * channels // width,)),
            pltpu.SemaphoreType.DMA(((members - 1) * 3 * depth // rest_rows,)),
            pltpu.SemaphoreType.DMA((2,)),
            pltpu.SemaphoreType.DMA((2,)),
            pltpu.SemaphoreType.DMA((2,)),
        ],
        compiler_params=params(),
        cost_estimate=cost(6 * rows * depth * channels, 2 * weights.size),
        name="load",
    )(me, x, weights, medium)


STRIP = 8


def strip_filter(scratch, i, start, taps, micro, back):
    total = None
    for lag, tap in enumerate(taps):
        first = start + micro * (lag if back else -lag)
        term = tap * scratch[i, pl.ds(first, STRIP, stride=micro), :]
        total = term if total is None else total + term
    return total


def group_masks(members, width):
    group = lax.broadcasted_iota(jnp.int32, (1, width), 1) % LANES // members
    return [jnp.where(group == g, 1.0, 0.0).astype(BF16) for g in range(LANES // members)]


def mixer_kernel(
    me_ref, w_ref, taps_ref, skip_ref, grad_ref, so_far_ref, first_ref, second_ref, *rest,
    members, micro, group, width
):
    x_refs = rest[: members - 1]
    (
        out_ref, so_far, grads, first, second, lagged, keys, values, mixed_grads, rounded,
        so_far_sem, grads_sem, first_sem, second_sem,
    ) = rest[members - 1 :]
    rows, channels = out_ref.shape[1:]
    depth = x_refs[0].shape[1]
    me = me_ref[0]
    length = rows // micro
    reach = taps_ref.shape[0] * LANES // 3 // channels
    tiles = channels // LANES
    spread = LANES // group * length
    window = width // group * length
    blocks = channels // width
    pairs = length // (2 * STRIP)
    margin = micro * STRIP
    masks = group_masks(group, micro * LANES)

    def block_copies(n):
        slot = n % 2
        lanes = pl.ds(pl.multiple_of(n * width, width), width)
        return (
            pltpu.make_async_copy(
                so_far_ref.at[:, :, lanes], so_far.at[slot], so_far_sem.at[slot]
            ),
            pltpu.make_async_copy(grad_ref.at[:, lanes], grads.at[slot], grads_sem.at[slot]),
        )

    def matrix_copies(n):
        wide = pl.ds(pl.multiple_of(n * window, window), window)
        return (
            pltpu.make_async_copy(first_ref.at[:, wide], first, first_sem),
            pltpu.make_async_copy(second_ref.at[:, wide], second, second_sem),
        )

    def lanes_of(n, tile):
        return pl.ds(pl.multiple_of(n * width + tile * LANES, LANES), LANES)

    def project(n):
        lanes = pl.ds(pl.multiple_of(n * width, width), width)
        for i in range(3):
            total = so_far[n % 2, i]
            for k, x_ref in enumerate(x_refs):
                row = pl.multiple_of(lax.rem(me + k + 1, members) * depth, depth)
                total = total + jnp.dot(
                    x_ref[...], w_ref[i, pl.ds(row, depth), lanes], preferred_element_type=F32
                )
            for tile in range(width // LANES):
                for b in range(micro):
                    for start in range(0, length, STRIP):
                        first_row = margin + micro * start + b
                        lagged[tile, i, pl.ds(first_row, STRIP, stride=micro), :] = total[
                            b * length + start : b * length + start + STRIP,
                            tile * LANES : (tile + 1) * LANES,
                        ]

    def forward(n, tile, taps):
        inner = slice(tile * LANES, (tile + 1) * LANES)
        scratch = lagged.at[tile]
        for b in range(micro):
            place = slice(b * LANES, (b + 1) * LANES)
            for pair in range(pairs):
                start = pair * 2 * STRIP
                span = slice(b * length + start, b * length + start + 2 * STRIP)
                upstream = grads[n % 2, span, inner].astype(F32)
                products, backs = [], []
                for half in range(2):
                    time = start + half * STRIP
                    query, key, value = (
                        strip_filter(scratch, i, margin + micro * time + b, taps[i], micro, False)
                        for i in range(3)
                    )
                    mixed_grad = upstream[half * STRIP : (half + 1) * STRIP] * query
                    own = slice(b * length + time, b * length + time + STRIP)
                    keys[own, inner] = key
                    values[own, inner] = value
                    mixed_grads[own, inner] = mixed_grad
                    products.append(key * value)
                    backs.append(mixed_grad)
                held_rows = slice(start, start + 2 * STRIP)
                rounded[0, tile, held_rows, place] = jnp.concatenate(products, axis=0).astype(BF16)
                rounded[1, tile, held_rows, place] = jnp.concatenate(backs, axis=0).astype(BF16)

    def medium(tile):
        places = slice(tile * spread, (tile + 1) * spread)
        return [
            jnp.dot(
                matrix[:, places],
                jnp.concatenate([rounded[turn, tile] * mask for mask in masks], axis=0),
                preferred_element_type=F32,
            )
            for turn, matrix in enumerate((first, second))
        ]

    def backward(n, tile, taps, mixed, product_grad):
        inner = slice(tile * LANES, (tile + 1) * LANES)
        lanes = lanes_of(n, tile)
        scratch = lagged.at[tile]
        skip = jnp.broadcast_to(skip_ref[0:1, lanes], (STRIP, LANES))
        for b in range(micro):
            place = slice(b * LANES, (b + 1) * LANES)
            for pair in range(pairs):
                start = pair * 2 * STRIP
                span = slice(b * length + start, b * length + start + 2 * STRIP)
                upstream = grads[n % 2, span, inner].astype(F32)
                for half in range(2):
                    time = start + half * STRIP
                    own = slice(b * length + time, b * length + time + STRIP)
                    here = slice(time, time + STRIP)
                    key, value = keys[own, inner], values[own, inner]
                    back = product_grad[here, place] + skip * mixed_grads[own, inner]
                    streams = (
                        upstream[half * STRIP : (half + 1) * STRIP]
                        * (mixed[here, place] + skip * (key * value)),
                        back * value,
                        back * key,
                    )
                    for i in range(3):
                        first_row = margin + micro * time + b
                        scratch[i, pl.ds(first_row, STRIP, stride=micro), :] = streams[i]
        for b in range(micro):
            for start in range(0, length, 2 * STRIP):
                span = slice(b * length + start, b * length + start + 2 * STRIP)
                for i in range(3):
                    strips = [
                        strip_filter(
                            scratch, i, margin + micro * (start + half) + b, taps[i], micro, True
                        )
                        for half in (0, STRIP)
                    ]
                    out_ref[i, span, lanes] = jnp.concatenate(strips, axis=0).astype(BF16)

    for copy in block_copies(0):
        copy.start()
    zeros = jnp.zeros((width // LANES, 3, margin, LANES), F32)
    lagged[:, :, :margin, :] = zeros
    lagged[:, :, margin + micro * length :, :] = zeros

    def step(n, carry):
        @pl.when(n + 1 < blocks)
        def _():
            for copy in block_copies(n + 1):
                copy.start()

        for copy in matrix_copies(n):
            copy.start()
        for copy in block_copies(n):
            copy.wait()
        taps = []
        for tile in range(width // LANES):
            line = n * (width // LANES) + tile
            taps.append([
                [
                    jnp.broadcast_to(
                        taps_ref[pl.ds((j * 3 + i) * tiles + line, 1), :], (STRIP, LANES)
                    )
                    for j in range(reach)
                ]
                for i in range(3)
            ])
        project(n)
        for tile in range(width // LANES):
            forward(n, tile, taps[tile])
        for copy in matrix_copies(n):
            copy.wait()
        for tile in range(width // LANES):
            backward(n, tile, taps[tile], *medium(tile))
        return carry

    lax.fori_loop(0, blocks, step, 0)


def mixer(me, weights, taps, skip, grad, so_far, first, second, others, micro):
    rows, channels = so_far.shape[1:]
    members = len(others) + 1
    length = rows // micro
    groups = first.shape[1] // length
    group = channels // groups
    width = min(256, channels)
    window = width // group * length
    tiles = width // LANES
    return pl.pallas_call(
        functools.partial(
            mixer_kernel, members=members, micro=micro, group=group, width=width
        ),
        in_specs=[IN_SMEM] + [IN_VMEM] * 3 + [ANYWHERE] * 4 + [IN_VMEM] * len(others),
        out_specs=IN_VMEM,
        out_shape=pltpu.VMEM(so_far.shape, BF16),
        scratch_shapes=[
            pltpu.VMEM((2, 3, rows, width), F32),
            pltpu.VMEM((2, rows, width), BF16),
            pltpu.VMEM((length, window), BF16),
            pltpu.VMEM((length, window), BF16),
            pltpu.VMEM((tiles, 3, micro * (length + 2 * STRIP), LANES), F32),
            pltpu.VMEM((rows, width), F32),
            pltpu.VMEM((rows, width), F32),
            pltpu.VMEM((rows, width), F32),
            pltpu.VMEM((2, tiles, length, micro * LANES), BF16),
            pltpu.SemaphoreType.DMA((2,)),
            pltpu.SemaphoreType.DMA((2,)),
            pltpu.SemaphoreType.DMA,
            pltpu.SemaphoreType.DMA,
        ],
        compiler_params=params(),
        cost_estimate=cost(0, 18 * rows * channels),
        name="mixer",
    )(me, held(weights), taps, skip, grad, so_far, first, second, *map(held, others))


def input_grad_kernel(member_ref, conv_ref, w_ref, *rest, first, depth, width, with_grad):
    start = member_ref[0] * depth + first
    if with_grad:
        out_ref, grad, grad_sem = rest[-3:]
        columns = slice(first, first + out_ref.shape[1])
        grad_copy = pltpu.make_async_copy(rest[0].at[:, columns], grad, grad_sem)
        grad_copy.start()
    else:
        out_ref = rest[-1]
    for step in range(out_ref.shape[1] // width):
        place = slice(step * width, (step + 1) * width)
        row = pl.multiple_of(start + step * width, width)
        total = None
        for i in range(3):
            term = lax.dot_general(
                w_ref[i, pl.ds(row, width), :],
                conv_ref[i],
                (((1,), (1,)), ((), ())),
                preferred_element_type=F32,
            )
            total = term if total is None else total + term
        total = total.T
        if with_grad:
            if step == 0:
                grad_copy.wait()
            total = total + grad[:, place].astype(F32)
        out_ref[:, place] = total.astype(BF16)


def input_grad(conv, weights, member, first, extent, depth, grad=None, after=()):
    rows = conv.shape[1]
    operands = [conv, weights] + ([] if grad is None else [grad])
    return pl.pallas_call(
        functools.partial(
            input_grad_kernel, first=first, depth=depth, width=SPAN, with_grad=grad is not None
        ),
        in_specs=[IN_SMEM, IN_VMEM, IN_VMEM]
        + [ANYWHERE] * (len(operands) - 2)
        + [IN_VMEM] * len(after),
        out_specs=IN_VMEM,
        out_shape=jax.ShapeDtypeStruct((rows, extent), BF16),
        scratch_shapes=[]
        if grad is None
        else [pltpu.VMEM((rows, extent), BF16), pltpu.SemaphoreType.DMA],
        compiler_params=params(),
        cost_estimate=cost(1, 1),
        name="input_grad",
    )(member, held(conv), held(weights), *operands[2:], *map(held, after))


def join(pieces, depth):
    rows = pieces[0][1].shape[0]

    def kernel(*refs):
        out_ref = refs[-1]
        for start in range(0, depth, SPAN):
            total = None
            for (first, piece), ref in zip(pieces, refs):
                if first <= start < first + piece.shape[1]:
                    term = ref[:, start - first : start - first + SPAN].astype(F32)
                    total = term if total is None else total + term
            out_ref[:, start : start + SPAN] = total.astype(BF16)

    return pl.pallas_call(
        kernel,
        out_shape=jax.ShapeDtypeStruct((rows, depth), BF16),
        compiler_params=params(),
        cost_estimate=cost(0, 6 * rows * depth),
        name="join",
    )(*[piece for _, piece in pieces])


def cuts_of(eighths, depth):
    step = depth // 8
    if step % SPAN:
        return [(0, depth)]
    first, spans = 0, []
    for count in eighths:
        spans.append((first, count * step))
        first += count * step
    return spans


def local(block_input, incoming, in_weight, short_taps, medium_taps, skip_weight):
    micro, length, depth = block_input.shape[1:]
    rows = micro * length
    members = lax.axis_size("tp")
    sections = lax.axis_size("section")
    me = lax.axis_index("tp")
    weights = jnp.transpose(in_weight[0], (1, 0, 2))
    x = block_input.reshape(rows, depth)
    grad = incoming.reshape(rows, depth)

    def owner(step):
        return jnp.full((1,), lax.rem(me + step, members), jnp.int32)

    others = []
    for k in range(1, members):
        pairs = [((m + k) % members, m) for m in range(members)]
        others.append(lax.ppermute(x, "tp", pairs))
    weights, so_far, first, second = load(owner(0), x, weights, medium_taps[0], members)
    conv = mixer(
        owner(0), weights, short_taps.reshape(-1, LANES), skip_weight, grad, so_far, first,
        second, others, micro,
    )
    pieces = []
    for k in list(range(1, members)) + [0]:
        pairs = [
            (s * members + m, (s - 1) % sections * members + (m + k) % members)
            for s in range(sections)
            for m in range(members)
        ]
        cuts = cuts_of(AWAY_CUTS if k else OWN_CUTS, depth)
        for first_column, extent in cuts:
            last = k == 0 and first_column + extent == depth and members > 1
            share = input_grad(
                conv, weights, owner(k), first_column, extent, depth,
                None if k else grad, (pieces[0][1],) if last else (),
            )
            pieces.append((first_column, lax.ppermute(share, ("section", "tp"), pairs)))
    return join(pieces, depth).reshape(block_input.shape)


def solution(mesh):
    in_specs = (
        P("section", None, None, "tp"),
        P("section", None, None, "tp"),
        P("section", None, None, "tp"),
        P("section", None, None, "tp"),
        P("section", None, "tp"),
        P("section", "tp"),
    )
    out_specs = P("section", None, None, "tp")
    return jax.shard_map(local, mesh=mesh, in_specs=in_specs, out_specs=out_specs, check_vma=False)
```
